256 devices in a mesh: grp: 8 (over y, z_hi), dev: 32 (over x, z_lo, core).
Axes of the slice: x: 4, y: 4, z: 8 (z_hi: 2, z_lo: 4; z = z_hi * 4 + z_lo), core: 2. Of those that a mesh axis runs over, the one named last changes fastest.
Arguments:
- doc_states: bfloat16 [2048, 128, 768], P(('grp', 'dev')), parts along dimension 0
- context_embeds: bfloat16 [4096, 768], P(('grp', 'dev')), parts along dimension 0
- w_qkv: bfloat16 [768, 2304], P('dev'), may hold values from -0.21875 to 0.21875
- w_out: bfloat16 [768, 768], P('dev'), may hold values from -0.21875 to 0.21875
- ln_gain: float32 [768], replicated, may hold values from 0.1 to 1.9
- queries: bfloat16 [2048, 768], P(('grp', 'dev')), parts along dimension 0
- positive: int32 [2048], P(('grp', 'dev')), parts along dimension 0, may hold values from 0 to 255, each once
- lengths: int32 [2048], P(('grp', 'dev')), parts along dimension 0, may hold values from 32 to 128, as said below
Outputs:
- doc_embed: bfloat16 [2048, 768], P(('grp', 'dev')), parts along dimension 0
- doc_grad: float32 [2048, 768], P(('grp', 'dev')), parts along dimension 0
- query_grad: float32 [2048, 768], P(('grp', 'dev')), parts along dimension 0
- query_loss: float32 [2048], P(('grp', 'dev')), parts along dimension 0
The draws below stay inside these ranges and needn't reach their ends.
There are 8 independent parts, one for each index of `grp`. The reference program is written for one: setup_inputs(seed, part) draws one part's arguments, and reference() takes and returns one part's arrays. A program takes and returns all parts, laid end to end along the dimension named above; an argument that names none is the same for every part. Nothing has to cross between parts.
Inputs may be any that keep to these rules, and one draw needn't show every extreme that they name: `lengths`: every document has at least 32 valid tokens; the first document of the group has all 128.
All inputs are finite; a program needn't handle non-finite values.
Results may differ from the reference program's by a relative error of at most 0.0084.
Values may be sent and summed in bfloat16 or wider, within the bound.
No kernel may reach another device: no remote copies, remote signals or barrier semaphores. Data moves between devices by JAX's collectives and lax.ppermute only.
A program may use at most 64 MiB of HBM per device.

```python
import jax
import jax.numpy as jnp
from jax import lax

HIDDEN_DIMENSION = 768
HEADS = 12
HEAD_DIM = 64
SEQ = 128
DOCS = 256
CTX = 512


def draw_doc_states(key, part):
    key = jax.random.fold_in(key, 11)
    values = jax.random.normal(key, (DOCS, SEQ, HIDDEN_DIMENSION), jnp.float32)
    return values.astype(jnp.bfloat16)


def draw_context_embeds(key, part):
    key = jax.random.fold_in(key, 23)
    values = jax.random.normal(key, (CTX, HIDDEN_DIMENSION), jnp.float32)
    return values.astype(jnp.bfloat16)


def draw_queries(key, part):
    key = jax.random.fold_in(key, 37)
    values = jax.random.normal(key, (DOCS, HIDDEN_DIMENSION), jnp.float32)
    return values.astype(jnp.bfloat16)


def draw_lengths(key, part):
    key = jax.random.fold_in(key, 41)
    values = jax.random.randint(key, (DOCS,), SEQ // 4, SEQ + 1, jnp.int32)
    return values.at[0].set(SEQ)


def level_of(stream_key, dims, cuts, least, largest):
    factor_of = 1.0
    for dim, blocks in cuts:
        steps = jax.random.uniform(jax.random.fold_in(jax.random.fold_in(stream_key, 6), dim), (blocks,), jnp.float32, least / len(cuts), largest / len(cuts))
        factor_of = factor_of * jnp.repeat(jnp.exp(steps), dims[dim] // blocks).reshape((-1,) + (1,) * (len(dims) - 1 - dim))
    return factor_of


def centred(own_key, shape, scale, reach, shards=(), kind=jnp.bfloat16):
    drawn = jax.random.normal(own_key, shape, jnp.float32) * scale
    if len(shards) > 0:
        drawn = level_of(own_key, shape, shards, -0.22, 0.18) * drawn
    return jnp.clip(drawn, min=-reach, max=reach).astype(kind)


def setup_inputs(seed: int = 0, part: int = 0) -> dict:
    keys = jax.random.split(jax.random.key(seed), 9)
    part_keys = jax.random.split(jax.random.fold_in(keys[8], part), 9)
    return {
        "doc_states": draw_doc_states(jax.random.fold_in(jax.random.fold_in(keys[8], part), 71), part),
        "context_embeds": draw_context_embeds(jax.random.fold_in(jax.random.fold_in(keys[8], part), 71), part),
        "w_qkv": centred(keys[2], (HIDDEN_DIMENSION, 3 * HIDDEN_DIMENSION), HIDDEN_DIMENSION ** -0.5, 0.21875, ((0, 32),)),
        "w_out": centred(keys[3], (HIDDEN_DIMENSION, HIDDEN_DIMENSION), HIDDEN_DIMENSION ** -0.5, 0.21875, ((0, 32),)),
        "ln_gain": jnp.clip(1.0 + 0.18 * jax.random.normal(keys[4], (HIDDEN_DIMENSION,), jnp.float32), 0.1, 1.9),
        "queries": draw_queries(jax.random.fold_in(jax.random.fold_in(keys[8], part), 71), part),
        "positive": jax.random.permutation(part_keys[6], DOCS).astype(jnp.int32),
        "lengths": draw_lengths(jax.random.fold_in(jax.random.fold_in(keys[8], part), 71), part),
    }


contrastive_sharpness = 0.25
epsilon = 1e-05

def reference(doc_states, context_embeds, w_qkv, w_out, ln_gain, queries, positive, lengths):
    context_kv = jnp.dot(context_embeds, w_qkv[:, HIDDEN_DIMENSION:], preferred_element_type=jnp.float32).astype(jnp.bfloat16)
    ctx_keys = context_kv[:, :HIDDEN_DIMENSION].astype(jnp.float32).reshape(CTX, HEADS, HEAD_DIM)
    ctx_values = context_kv[:, HIDDEN_DIMENSION:].astype(jnp.float32).reshape(CTX, HEADS, HEAD_DIM)
    multiplier = 1.0 / HEAD_DIM ** 0.5

    def encode(inputs):
        states, length = inputs
        qkv = jnp.dot(states, w_qkv, preferred_element_type=jnp.float32).astype(jnp.bfloat16)
        qkv = qkv.astype(jnp.float32).reshape(SEQ, 3, HEADS, HEAD_DIM)
        query_part = qkv[:, 0]
        key_part = qkv[:, 1]
        value_part = qkv[:, 2]
        valid = jnp.arange(SEQ) < length
        score_ctx = jnp.einsum('shd,chd->hsc', query_part, ctx_keys) * multiplier
        score_own = jnp.einsum('shd,thd->hst', query_part, key_part) * multiplier
        score_own = jnp.where(valid[None, None, :], score_own, -jnp.inf)
        joined = jnp.concatenate([score_ctx, score_own], axis=-1)
        highest = lax.optimization_barrier(jnp.max(joined, axis=-1, keepdims=True))
        expo = jnp.exp(joined - highest)
        probs = (expo / lax.optimization_barrier(jnp.sum(expo, axis=-1, keepdims=True))).astype(jnp.bfloat16).astype(jnp.float32)
        mixed = jnp.einsum('hsc,chd->shd', probs[..., :CTX], ctx_values)
        mixed = mixed + jnp.einsum('hst,thd->shd', probs[..., CTX:], value_part)
        attn = mixed.reshape(SEQ, HIDDEN_DIMENSION).astype(jnp.bfloat16)
        hidden = states.astype(jnp.float32) + jnp.dot(attn, w_out, preferred_element_type=jnp.float32)
        center = lax.optimization_barrier(jnp.mean(hidden, axis=-1, keepdims=True))
        spread = lax.optimization_barrier(jnp.mean((hidden - center) ** 2, axis=-1, keepdims=True))
        normed = (hidden - center) / jnp.sqrt(spread + epsilon) * ln_gain
        pooled = lax.optimization_barrier(jnp.sum(jnp.where(valid[:, None], normed, 0.0), axis=0)) / length.astype(jnp.float32)
        return pooled.astype(jnp.bfloat16)
    doc_embed = lax.map(encode, (doc_states, lengths))
    logit_divisor = 1.0 / (HIDDEN_DIMENSION ** 0.5 * contrastive_sharpness)
    scores = jnp.dot(queries, doc_embed.T, preferred_element_type=jnp.float32) * logit_divisor
    highest = lax.optimization_barrier(jnp.max(scores, axis=1, keepdims=True))
    lse = highest[:, 0] + jnp.log(lax.optimization_barrier(jnp.sum(jnp.exp(scores - highest), axis=1)))
    is_positive = jnp.arange(DOCS, dtype=jnp.int32)[None, :] == positive[:, None]
    query_loss = lse - lax.optimization_barrier(jnp.sum(jnp.where(is_positive, scores, 0.0), axis=1))
    coeff = jnp.exp(scores - lse[:, None]) - is_positive.astype(jnp.float32)
    doc_grad = jnp.dot(coeff.T, queries.astype(jnp.float32), precision=lax.Precision.HIGHEST) * logit_divisor
    query_grad = jnp.dot(coeff, doc_embed.astype(jnp.float32), precision=lax.Precision.HIGHEST) * logit_divisor
    return (doc_embed, doc_grad, query_grad, query_loss)
```

```python
import functools

import jax
import jax.numpy as jnp
from jax import lax
from jax.experimental import pallas as pl
from jax.experimental.pallas import tpu as pltpu
from jax.sharding import PartitionSpec as P

HEAD = 64
PAIR = 128
SHARPNESS = 0.25
EPSILON = 1e-5
LOG2E = 1.4426950408889634
F32 = jnp.float32
BF16 = jnp.bfloat16
VMEM_LIMIT = 56 * 2**20
NT = (((1,), (1,)), ((), ()))


def halves(tile):
    low = lax.broadcasted_iota(jnp.int32, (1, PAIR), 1) < HEAD
    zero = jnp.zeros_like(tile)
    return jnp.where(low, tile, zero).astype(BF16), jnp.where(low, zero, tile).astype(BF16)


def ones_beside(rows):
    low = lax.broadcasted_iota(jnp.int32, (1, PAIR), 1) < HEAD
    first = lax.broadcasted_iota(jnp.int32, (2 * rows, 1), 0) < rows
    return jnp.where(jnp.logical_xor(first, low), 0.0, 1.0).astype(BF16)


def attend_kernel(rows, unroll, len_ref, x_ref, ctx_ref, w_ref, o_ref, q_s, k_s, v_s, kc_s, vc_s):
    pairs, docs, two_seq, _ = k_s.shape
    seq = two_seq // 2
    width = pairs * PAIR
    blocks, ctx_rows, hidden = ctx_ref.shape
    nctx = blocks * 16
    scale = LOG2E / HEAD**0.5

    def project(i, _):
        r = pl.ds(pl.multiple_of(i * rows, rows), rows)
        states = x_ref[r, :]
        q = jnp.dot(states, w_ref[:, :width], preferred_element_type=F32)
        q_s[r, :] = (q * scale).astype(BF16)
        for begin, out in ((width, k_s), (2 * width, v_s)):
            t = jnp.dot(states, w_ref[:, begin : begin + width], preferred_element_type=F32)
            for j in range(pairs):
                even, odd = halves(t[:, j * PAIR : (j + 1) * PAIR])
                for e in range(rows // seq):
                    d = i * (rows // seq) + e
                    out[j, d, :seq] = even[e * seq : (e + 1) * seq]
                    out[j, d, seq:] = odd[e * seq : (e + 1) * seq]
        return 0

    lax.fori_loop(0, docs * seq // rows, project, 0)
    ctx = ctx_ref[:, :16, :].reshape(nctx, hidden)
    for begin, out in ((width, kc_s), (2 * width, vc_s)):
        t = jnp.dot(ctx, w_ref[:, begin : begin + width], preferred_element_type=F32)
        for j in range(pairs):
            even, odd = halves(t[:, j * PAIR : (j + 1) * PAIR])
            out[j, :nctx] = even
            out[j, nctx:] = odd
    ones_ctx = ones_beside(nctx)
    ones_own = ones_beside(seq)
    slot = lax.broadcasted_iota(jnp.int32, (1, 2 * seq), 1)
    slot = jnp.where(slot < seq, slot, slot - seq)
    for j in range(pairs):

        def doc(d, _):
            r = pl.ds(pl.multiple_of(d * seq, seq), seq)
            q = q_s[r, j * PAIR : (j + 1) * PAIR]
            bias = jnp.where(slot < len_ref[d], 0.0, -jnp.inf).astype(F32)
            score_ctx = lax.dot_general(q, kc_s[j], NT, preferred_element_type=F32)
            score_own = lax.dot_general(q, k_s[j, d], NT, preferred_element_type=F32) + bias
            p_ctx, p_own = [], []
            for e in range(2):
                c = score_ctx[:, e * nctx : (e + 1) * nctx]
                o = score_own[:, e * seq : (e + 1) * seq]
                top = jnp.maximum(jnp.max(c, axis=1, keepdims=True), jnp.max(o, axis=1, keepdims=True))
                p_ctx.append(jnp.exp2(c - top).astype(BF16))
                p_own.append(jnp.exp2(o - top).astype(BF16))
            mixed = jnp.dot(
                jnp.concatenate(p_ctx, axis=1),
                jnp.concatenate([vc_s[j], ones_ctx], axis=1),
                preferred_element_type=F32,
            ) + jnp.dot(
                jnp.concatenate(p_own, axis=1),
                jnp.concatenate([v_s[j, d], ones_own], axis=1),
                preferred_element_type=F32,
            )
            o_ref[r, j * PAIR : (j + 1) * PAIR] = (mixed[:, :PAIR] / mixed[:, PAIR:]).astype(BF16)
            return 0

        lax.fori_loop(0, docs, doc, 0, unroll=unroll)


def attend(lengths, x, ctx, w, seq):
    tokens, hidden = x.shape
    docs = tokens // seq
    width = w.shape[1] // 3
    pairs = width // PAIR
    nctx = ctx.shape[0] * 16
    vmem = pl.BlockSpec(memory_space=pltpu.VMEM)
    flops = 2 * tokens * hidden * 3 * width + 2 * nctx * hidden * 2 * width + 4 * tokens * (nctx + seq) * width
    return pl.pallas_call(
        functools.partial(attend_kernel, 2 * seq, docs),
        out_shape=jax.ShapeDtypeStruct((tokens, width), BF16),
        in_specs=[pl.BlockSpec(memory_space=pltpu.SMEM), vmem, vmem, vmem],
        out_specs=vmem,
        scratch_shapes=[
            pltpu.VMEM((tokens, width), BF16),
            pltpu.VMEM((pairs, docs, 2 * seq, PAIR), BF16),
            pltpu.VMEM((pairs, docs, 2 * seq, PAIR), BF16),
            pltpu.VMEM((pairs, 2 * nctx, PAIR), BF16),
            pltpu.VMEM((pairs, 2 * nctx, PAIR), BF16),
        ],
        compiler_params=pltpu.CompilerParams(vmem_limit_bytes=VMEM_LIMIT),
        cost_estimate=pl.CostEstimate(flops=flops, bytes_accessed=8 * 2**20, transcendentals=tokens * (nctx + seq) * 2 * pairs),
        name="attend",
    )(lengths, x, ctx, w)


def pool_kernel(seq, len_ref, x_ref, attn_ref, w_ref, gain_ref, o_ref):
    docs = o_ref.shape[0]
    hidden = x_ref.shape[1]
    position = lax.broadcasted_iota(jnp.int32, (seq, 1), 0)
    pooled = []
    for d in range(docs):
        r = slice(d * seq, (d + 1) * seq)
        h = x_ref[r, :].astype(F32) + jnp.dot(attn_ref[r, :], w_ref[...], preferred_element_type=F32)
        center = jnp.mean(h, axis=1, keepdims=True)
        off = h - center
        spread = jnp.mean(off * off, axis=1, keepdims=True)
        length = len_ref[d]
        weight = jnp.where(position < length, lax.rsqrt(spread + EPSILON), 0.0)
        pooled.append(jnp.sum(off * weight, axis=0, keepdims=True) / length.astype(F32))
    o_ref[...] = (jnp.concatenate(pooled, axis=0) * gain_ref[...]).astype(BF16)


def pool(lengths, x, attn, w_out, gain, seq):
    tokens, hidden = x.shape
    vmem = pl.BlockSpec(memory_space=pltpu.VMEM)
    return pl.pallas_call(
        functools.partial(pool_kernel, seq),
        out_shape=jax.ShapeDtypeStruct((tokens // seq, hidden), BF16),
        in_specs=[pl.BlockSpec(memory_space=pltpu.SMEM), vmem, vmem, vmem, vmem],
        out_specs=vmem,
        compiler_params=pltpu.CompilerParams(vmem_limit_bytes=VMEM_LIMIT),
        cost_estimate=pl.CostEstimate(flops=2 * tokens * hidden * hidden, bytes_accessed=5 * 2**20, transcendentals=0),
        name="pool",
    )(lengths, x, attn, w_out, gain.reshape(1, hidden))


def exact_dot(a, b):
    a1 = a.astype(BF16)
    rest = a - a1.astype(F32)
    a2 = rest.astype(BF16)
    a3 = (rest - a2.astype(F32)).astype(BF16)
    n = a.shape[0]
    out = jnp.dot(jnp.concatenate([a1, a2, a3], axis=0), b, preferred_element_type=F32)
    return out[:n] + out[n : 2 * n] + out[2 * n :]


def contrast_kernel(me_ref, pack_ref, embed_ref, dgrad_ref, qgrad_ref, loss_ref, coeff_s):
    blocks, rows, hidden = pack_ref.shape
    docs = embed_ref.shape[0]
    mine = docs // blocks
    cols = blocks * 16
    me = me_ref[0]
    divisor = 1.0 / (hidden**0.5 * SHARPNESS)
    packed = pack_ref[:, 16:, :].reshape(cols, hidden)
    embed = embed_ref[...]
    lane = lax.broadcasted_iota(jnp.int32, (1, cols), 1)
    picker = jnp.where(lane % 16 == mine, 1.0, 0.0) * jnp.ones((16, 1), F32)
    positive = jnp.dot(picker.astype(BF16), packed[:, :cols], preferred_element_type=F32)[:1]
    scores_t = lax.dot_general(embed, packed, NT, preferred_element_type=F32) * divisor
    top = jnp.max(scores_t, axis=0, keepdims=True)
    lse_t = top + jnp.log(jnp.sum(jnp.exp(scores_t - top), axis=0, keepdims=True))
    doc_id = lax.broadcasted_iota(jnp.int32, (docs, 1), 0).astype(F32)
    coeff_t = jnp.exp(scores_t - lse_t) - jnp.where(doc_id == positive, 1.0, 0.0)
    coeff_s[...] = jnp.where(lane % 16 < mine, coeff_t, 0.0)
    own_t = coeff_s[pl.ds(pl.multiple_of(me * mine, mine), mine), :]
    dgrad_ref[...] = exact_dot(own_t, packed) * divisor
    queries = pack_ref[pl.ds(me, 1), 16:, :].reshape(16, hidden)
    scores = lax.dot_general(queries, embed, NT, preferred_element_type=F32) * divisor
    top = jnp.max(scores, axis=1, keepdims=True)
    lse = top + jnp.log(jnp.sum(jnp.exp(scores - top), axis=1, keepdims=True))
    row = lax.broadcasted_iota(jnp.int32, (16, 1), 0)
    own_positive = jnp.sum(jnp.where(lane == me * 16 + row, positive, 0.0), axis=1, keepdims=True)
    is_positive = lax.broadcasted_iota(jnp.int32, (1, docs), 1).astype(F32) == own_positive
    loss = lse - jnp.sum(jnp.where(is_positive, scores, 0.0), axis=1, keepdims=True)
    coeff = jnp.exp(scores - lse) - jnp.where(is_positive, 1.0, 0.0)
    qgrad_ref[...] = exact_dot(coeff, embed)[:mine] * divisor
    spot = lax.broadcasted_iota(jnp.int32, (1, PAIR), 1)
    loss_ref[...] = jnp.sum(jnp.where(spot == row, loss, 0.0), axis=0, keepdims=True)[:, :mine]


def contrast(me, pack, embed):
    blocks, rows, hidden = pack.shape
    docs = embed.shape[0]
    mine = docs // blocks
    vmem = pl.BlockSpec(memory_space=pltpu.VMEM)
    return pl.pallas_call(
        contrast_kernel,
        out_shape=(
            jax.ShapeDtypeStruct((mine, hidden), F32),
            jax.ShapeDtypeStruct((mine, hidden), F32),
            jax.ShapeDtypeStruct((1, mine), F32),
        ),
        in_specs=[pl.BlockSpec(memory_space=pltpu.SMEM), vmem, vmem],
        out_specs=(vmem, vmem, vmem),
        scratch_shapes=[pltpu.VMEM((docs, blocks * 16), F32)],
        compiler_params=pltpu.CompilerParams(vmem_limit_bytes=VMEM_LIMIT),
        name="contrast",
    )(me, pack, embed)


def spread_all(block, axis, size):
    return lax.all_to_all(jnp.broadcast_to(block[None], (size,) + block.shape), axis, 0, 0)


def pack_kernel(me_ref, positive_ref, context_ref, query_ref, o_ref):
    mine, hidden = query_ref.shape
    spot = lax.broadcasted_iota(jnp.int32, (8, hidden), 1) - 16 * me_ref[0]
    first = lax.broadcasted_iota(jnp.int32, (8, hidden), 0) == 0
    rows = jnp.zeros((8, hidden), F32)
    for i in range(mine):
        rows = jnp.where(jnp.logical_and(spot == i, first), positive_ref[i].astype(F32), rows)
    o_ref[:16] = context_ref[...]
    o_ref[16:] = jnp.concatenate([query_ref[...].astype(F32), rows], axis=0).astype(BF16)


def pack_rows(me, context, queries, positive):
    hidden = queries.shape[1]
    smem = pl.BlockSpec(memory_space=pltpu.SMEM)
    vmem = pl.BlockSpec(memory_space=pltpu.VMEM)
    return pl.pallas_call(
        pack_kernel,
        out_shape=jax.ShapeDtypeStruct((32, hidden), BF16),
        in_specs=[smem, smem, vmem, vmem],
        out_specs=vmem,
        name="pack",
    )(me, positive, context, queries)


def local(doc_states, context_embeds, w_qkv, w_out, ln_gain, queries, positive, lengths):
    docs, seq, hidden = doc_states.shape
    size = lax.axis_size("dev")
    me = lax.axis_index("dev")
    x = doc_states.reshape(docs * seq, hidden)
    pack = spread_all(pack_rows(me.reshape(1), context_embeds, queries, positive), "dev", size)
    weights = lax.all_gather(jnp.concatenate([w_qkv, w_out], axis=1), "dev", axis=0, tiled=True)
    attn = attend(lengths, x, pack, weights[:, : 3 * hidden], seq)
    embed = pool(lengths, x, attn, weights[:, 3 * hidden :], ln_gain, seq)
    embeds = spread_all(embed, "dev", size).reshape(size * docs, hidden)
    dgrad, qgrad, loss = contrast(me.reshape(1), pack, embeds)
    return embed, dgrad, qgrad, loss.reshape(docs)


def solution(mesh):
    both = ("grp", "dev")
    return jax.shard_map(
        local,
        mesh=mesh,
        in_specs=(
            P(both, None, None),
            P(both, None),
            P("dev", None),
            P("dev", None),
            P(),
            P(both, None),
            P(both),
            P(both),
        ),
        out_specs=(P(both, None), P(both, None), P(both, None), P(both)),
        check_vma=False,
    )
```

```python
import functools

import jax
import jax.numpy as jnp
from jax import lax
from jax.experimental import pallas as pl
from jax.experimental.pallas import tpu as pltpu
from jax.sharding import PartitionSpec as P

HEAD = 64
PAIR = 128
SHARPNESS = 0.25
EPSILON = 1e-5
LOG2E = 1.4426950408889634
F32 = jnp.float32
BF16 = jnp.bfloat16
VMEM_LIMIT = 56 * 2**20
NT = (((1,), (1,)), ((), ()))


def halves(tile):
    low = lax.broadcasted_iota(jnp.int32, (1, PAIR), 1) < HEAD
    zero = jnp.zeros_like(tile)
    return jnp.where(low, tile, zero).astype(BF16), jnp.where(low, zero, tile).astype(BF16)


def ones_beside(rows):
    low = lax.broadcasted_iota(jnp.int32, (1, PAIR), 1) < HEAD
    first = lax.broadcasted_iota(jnp.int32, (2 * rows, 1), 0) < rows
    return jnp.where(jnp.logical_xor(first, low), 0.0, 1.0).astype(BF16)


HALF = 384
WEIGHTS = 3 * HALF
PROJECT = 4 * HALF
ROWS = 5 * HALF
BLOCK = ROWS + 128
SMALL = ((0, 0), (2, 1), (0, 2), (2, 3))
LARGE = ((0, 0), (1, 0), (3, 0), (0, 1))


def half_block(half, positive_ref, context_ref, query_ref, wqkv_ref, wout_ref):
    mine, hidden = query_ref.shape
    first = half == 0
    parts = [wqkv_ref[:, b * hidden : (b + 1) * hidden].astype(F32) for b in range(3)] + [wout_ref[...].astype(F32)]
    parts.append(jnp.concatenate([context_ref[...].astype(F32), query_ref[...].astype(F32)], axis=0))
    parts = [jnp.where(first, p[:, :HALF], p[:, HALF:]) for p in parts]
    row = lax.broadcasted_iota(jnp.int32, (24, 128), 0)
    spot = jnp.zeros((24, 128), F32)
    for i in range(mine):
        spot = jnp.where(row == 16 + i, positive_ref[i].astype(F32), spot)
    return jnp.concatenate(parts + [spot], axis=1)


def give_kernel(spot_ref, positive_ref, context_ref, query_ref, wqkv_ref, wout_ref, o_ref):
    block = half_block(1 - spot_ref[1], positive_ref, context_ref, query_ref, wqkv_ref, wout_ref)
    o_ref[...] = block.astype(BF16)


def chip_kernel(spot_ref, positive_ref, context_ref, query_ref, wqkv_ref, wout_ref, got_ref, o_ref):
    own = half_block(spot_ref[1], positive_ref, context_ref, query_ref, wqkv_ref, wout_ref)
    got = got_ref[...].astype(F32)
    first = spot_ref[1] == 0
    low = jnp.where(first, own, got)
    high = jnp.where(first, got, own)
    o_ref[:, :PROJECT] = jnp.concatenate([low[:, :PROJECT], high[:, :PROJECT]], axis=0).astype(BF16)
    rows = [low[:16, PROJECT:], high[:16, PROJECT:], low[16:, PROJECT:], high[16:, PROJECT:]]
    o_ref[:, PROJECT:] = jnp.concatenate(rows, axis=0).astype(BF16)


def build(kernel, rows, name, spot, positive, *arrays):
    smem = pl.BlockSpec(memory_space=pltpu.SMEM)
    vmem = pl.BlockSpec(memory_space=pltpu.VMEM)
    return pl.pallas_call(
        kernel,
        out_shape=jax.ShapeDtypeStruct((rows, BLOCK), BF16),
        in_specs=[smem, smem] + [vmem] * len(arrays),
        out_specs=vmem,
        name=name,
    )(spot, positive, *arrays)


def layer_kernel(rows, unroll, len_ref, spot_ref, x_ref, gain_ref, *refs):
    pieces, refs = refs[:8], refs[8:]
    o_ref, told_ref, w_s, wo_s, ctx_s, query_s, spot_s, q_s, k_s, v_s, kc_s, vc_s, attn_s, sems = refs
    tokens, hidden = x_ref.shape
    docs = o_ref.shape[0]
    seq = tokens // docs
    pairs = hidden // PAIR
    per = HALF // PAIR
    nctx = ctx_s.shape[1] * ctx_s.shape[2]
    scale = LOG2E / HEAD**0.5
    x, core, z = spot_ref[0], spot_ref[1], spot_ref[2]
    weights, others, last = [], [], []
    for side in range(2):
        for p, (ax, az) in enumerate(LARGE):
            piece = pieces[side * 4 + p]
            n = side * 4 + p
            for k, (bx, bz) in enumerate(SMALL):
                at = pl.multiple_of((((x + ax + bx) & 3) * 4 + ((z + az + bz) & 3)) * 48, 48)
                here = (core + side) & 1
                lanes = pl.ds(pl.multiple_of(here * HALF, HALF), HALF)
                weights.append(
                    pltpu.make_async_copy(
                        piece.at[k, :, pl.ds(0, WEIGHTS)], w_s.at[side, pl.ds(at, 48)], sems.at[0, n * 4 + k]
                    )
                )
                last.append(
                    pltpu.make_async_copy(
                        piece.at[k, :, pl.ds(WEIGHTS, HALF)], wo_s.at[pl.ds(at, 48), lanes], sems.at[1, n * 4 + k]
                    )
                )
            others.append(
                pltpu.make_async_copy(
                    piece.at[:, pl.ds(0, 32), pl.ds(PROJECT, HALF)], ctx_s.at[side, pl.ds(4 * p, 4)], sems.at[2, n]
                )
            )
            last.append(
                pltpu.make_async_copy(
                    piece.at[:, pl.ds(32, 16), pl.ds(PROJECT, HALF)], query_s.at[side, pl.ds(4 * p, 4)], sems.at[2, 8 + n]
                )
            )
            if side == 0:
                last.append(
                    pltpu.make_async_copy(
                        piece.at[:, pl.ds(32, 16), pl.ds(ROWS, 128)], spot_s.at[pl.ds(4 * p, 4)], sems.at[2, 16 + n]
                    )
                )
    for copy in weights + others + last:
        copy.start()
    for copy in weights:
        copy.wait()

    def project(i, _):
        r = pl.ds(pl.multiple_of(i * rows, rows), rows)
        states = x_ref[r, :]
        for side in range(2):
            q = jnp.dot(states, w_s[side, :, :HALF], preferred_element_type=F32)
            q_s[r, side * HALF : (side + 1) * HALF] = (q * scale).astype(BF16)
            for begin, out in ((HALF, k_s), (2 * HALF, v_s)):
                t = jnp.dot(states, w_s[side, :, begin : begin + HALF], preferred_element_type=F32)
                for j in range(per):
                    even, odd = halves(t[:, j * PAIR : (j + 1) * PAIR])
                    for e in range(rows // seq):
                        d = i * (rows // seq) + e
                        out[side * per + j, d, :seq] = even[e * seq : (e + 1) * seq]
                        out[side * per + j, d, seq:] = odd[e * seq : (e + 1) * seq]
        return 0

    lax.fori_loop(0, tokens // rows, project, 0)
    for copy in others:
        copy.wait()
    near = ctx_s[0].reshape(nctx, HALF)
    far = ctx_s[1].reshape(nctx, HALF)
    first = core == 0
    ctx = jnp.concatenate([jnp.where(first, near, far), jnp.where(first, far, near)], axis=1)
    for side in range(2):
        for begin, out in ((HALF, kc_s), (2 * HALF, vc_s)):
            t = jnp.dot(ctx, w_s[side, :, begin : begin + HALF], preferred_element_type=F32)
            for j in range(per):
                even, odd = halves(t[:, j * PAIR : (j + 1) * PAIR])
                out[side * per + j, :nctx] = even
                out[side * per + j, nctx:] = odd
    ones_ctx = ones_beside(nctx)
    ones_own = ones_beside(seq)
    slot = lax.broadcasted_iota(jnp.int32, (1, 2 * seq), 1)
    slot = jnp.where(slot < seq, slot, slot - seq)
    for j in range(pairs):

        def doc(d, _):
            r = pl.ds(pl.multiple_of(d * seq, seq), seq)
            q = q_s[r, j * PAIR : (j + 1) * PAIR]
            bias = jnp.where(slot < len_ref[d], 0.0, -jnp.inf).astype(F32)
            score_ctx = lax.dot_general(q, kc_s[j], NT, preferred_element_type=F32)
            score_own = lax.dot_general(q, k_s[j, d], NT, preferred_element_type=F32) + bias
            p_ctx, p_own = [], []
            for e in range(2):
                c = score_ctx[:, e * nctx : (e + 1) * nctx]
                o = score_own[:, e * seq : (e + 1) * seq]
                top = jnp.maximum(jnp.max(c, axis=1, keepdims=True), jnp.max(o, axis=1, keepdims=True))
                p_ctx.append(jnp.exp2(c - top).astype(BF16))
                p_own.append(jnp.exp2(o - top).astype(BF16))
            mixed = jnp.dot(
                jnp.concatenate(p_ctx, axis=1),
                jnp.concatenate([vc_s[j], ones_ctx], axis=1),
                preferred_element_type=F32,
            ) + jnp.dot(
                jnp.concatenate(p_own, axis=1),
                jnp.concatenate([v_s[j, d], ones_own], axis=1),
                preferred_element_type=F32,
            )
            attn_s[r, j * PAIR : (j + 1) * PAIR] = (mixed[:, :PAIR] / mixed[:, PAIR:]).astype(BF16)
            return 0

        lax.fori_loop(0, docs, doc, 0, unroll=unroll)
    for copy in last:
        copy.wait()
    w_near = wo_s[pl.ds(pl.multiple_of(core * HALF, HALF), HALF), :]
    w_far = wo_s[pl.ds(pl.multiple_of((1 - core) * HALF, HALF), HALF), :]
    position = lax.broadcasted_iota(jnp.int32, (seq, 1), 0)
    pooled = []
    for d in range(docs):
        r = slice(d * seq, (d + 1) * seq)
        h = x_ref[r, :].astype(F32) + jnp.dot(attn_s[r, :HALF], w_near, preferred_element_type=F32)
        h = h + jnp.dot(attn_s[r, HALF:], w_far, preferred_element_type=F32)
        center = jnp.mean(h, axis=1, keepdims=True)
        off = h - center
        spread = jnp.mean(off * off, axis=1, keepdims=True)
        length = len_ref[d]
        weight = jnp.where(position < length, lax.rsqrt(spread + EPSILON), 0.0)
        pooled.append(jnp.sum(off * weight, axis=0, keepdims=True) / length.astype(F32))
    o_ref[...] = (jnp.concatenate(pooled, axis=0) * gain_ref[...]).astype(BF16)
    count = told_ref.shape[0]
    near = query_s[0].reshape(count, HALF)
    far = query_s[1].reshape(count, HALF)
    told_ref[:, :HALF] = jnp.where(first, near, far)
    told_ref[:, HALF:hidden] = jnp.where(first, far, near)
    told_ref[:, hidden:] = spot_s[...].reshape(count, 128)


def layer(lengths, spot, x, gain, pieces, seq):
    tokens, hidden = x.shape
    docs = tokens // seq
    pairs = hidden // PAIR
    chips = 16
    nctx = chips * 32
    vmem = pl.BlockSpec(memory_space=pltpu.VMEM)
    smem = pl.BlockSpec(memory_space=pltpu.SMEM)
    hbm = pl.BlockSpec(memory_space=pl.ANY)
    return pl.pallas_call(
        functools.partial(layer_kernel, 2 * seq, docs),
        out_shape=(
            jax.ShapeDtypeStruct((docs, hidden), BF16),
            jax.ShapeDtypeStruct((chips * 16, hidden + 128), BF16),
        ),
        in_specs=[smem, smem, vmem, vmem] + [hbm] * 8,
        out_specs=(vmem, vmem),
        scratch_shapes=[
            pltpu.VMEM((2, hidden, WEIGHTS), BF16),
            pltpu.VMEM((hidden, hidden), BF16),
            pltpu.VMEM((2, chips, 32, HALF), BF16),
            pltpu.VMEM((2, chips, 16, HALF), BF16),
            pltpu.VMEM((chips, 16, 128), BF16),
            pltpu.VMEM((tokens, hidden), BF16),
            pltpu.VMEM((pairs, docs, 2 * seq, PAIR), BF16),
            pltpu.VMEM((pairs, docs, 2 * seq, PAIR), BF16),
            pltpu.VMEM((pairs, 2 * nctx, PAIR), BF16),
            pltpu.VMEM((pairs, 2 * nctx, PAIR), BF16),
            pltpu.VMEM((tokens, hidden), BF16),
            pltpu.SemaphoreType.DMA((3, 32)),
        ],
        compiler_params=pltpu.CompilerParams(vmem_limit_bytes=VMEM_LIMIT),
        name="layer",
    )(lengths, spot, x, gain.reshape(1, hidden), *pieces)


def exact_dot(a, b):
    a1 = a.astype(BF16)
    rest = a - a1.astype(F32)
    a2 = rest.astype(BF16)
    a3 = (rest - a2.astype(F32)).astype(BF16)
    n = a.shape[0]
    out = jnp.dot(jnp.concatenate([a1, a2, a3], axis=0), b, preferred_element_type=F32)
    return out[:n] + out[n : 2 * n] + out[2 * n :]


def contrast_kernel(spot_ref, told_ref, embed_ref, dgrad_ref, qgrad_ref, loss_ref, coeff_s, rows_s, loss_s):
    count = told_ref.shape[0]
    docs, hidden = embed_ref.shape
    mine = dgrad_ref.shape[0]
    divisor = 1.0 / (hidden**0.5 * SHARPNESS)
    core = spot_ref[1]
    queries = told_ref[:, :hidden]
    embed = embed_ref[...]
    beside = told_ref[:, hidden:].astype(F32)
    positive = beside.T[:1]
    scores_t = lax.dot_general(embed, queries, NT, preferred_element_type=F32) * divisor
    top = jnp.max(scores_t, axis=0, keepdims=True)
    lse_t = top + jnp.log(jnp.sum(jnp.exp(scores_t - top), axis=0, keepdims=True))
    doc_id = lax.broadcasted_iota(jnp.int32, (docs, 1), 0).astype(F32)
    coeff_s[...] = jnp.exp(scores_t - lse_t) - jnp.where(doc_id == positive, 1.0, 0.0)
    own = pl.multiple_of(((spot_ref[0] * 4 + spot_ref[2]) * 2 + core) * mine, mine)
    dgrad_ref[...] = exact_dot(coeff_s[pl.ds(own, mine), :], queries) * divisor
    scores = lax.dot_general(queries[:16], embed, NT, preferred_element_type=F32) * divisor
    top = jnp.max(scores, axis=1, keepdims=True)
    lse = top + jnp.log(jnp.sum(jnp.exp(scores - top), axis=1, keepdims=True))
    is_positive = lax.broadcasted_iota(jnp.int32, (1, docs), 1).astype(F32) == beside[:16, :1]
    loss = lse - jnp.sum(jnp.where(is_positive, scores, 0.0), axis=1, keepdims=True)
    rows_s[...] = jnp.exp(scores - lse) - jnp.where(is_positive, 1.0, 0.0)
    half = pl.ds(pl.multiple_of(core * mine, mine), mine)
    qgrad_ref[...] = exact_dot(rows_s[half, :], embed) * divisor
    loss_s[...] = jnp.broadcast_to(loss, loss_s.shape)
    spot = lax.broadcasted_iota(jnp.int32, (mine, 128), 1)
    row = lax.broadcasted_iota(jnp.int32, (mine, 128), 0)
    loss_ref[...] = jnp.sum(jnp.where(spot == row, loss_s[half, :], 0.0), axis=0, keepdims=True)[:, :mine]


def contrast(spot, told, embed, mine):
    count = told.shape[0]
    docs, hidden = embed.shape
    vmem = pl.BlockSpec(memory_space=pltpu.VMEM)
    return pl.pallas_call(
        contrast_kernel,
        out_shape=(
            jax.ShapeDtypeStruct((mine, hidden), F32),
            jax.ShapeDtypeStruct((mine, hidden), F32),
            jax.ShapeDtypeStruct((1, mine), F32),
        ),
        in_specs=[pl.BlockSpec(memory_space=pltpu.SMEM), vmem, vmem],
        out_specs=(vmem, vmem, vmem),
        scratch_shapes=[
            pltpu.VMEM((docs, count), F32),
            pltpu.VMEM((16, docs), F32),
            pltpu.VMEM((16, 128), F32),
        ],
        compiler_params=pltpu.CompilerParams(vmem_limit_bytes=VMEM_LIMIT),
        name="contrast",
    )(spot, told, embed)


def spread_all(block, axis, size):
    return lax.all_to_all(jnp.broadcast_to(block[None], (size,) + block.shape), axis, 0, 0)


def fetch(value, dx=0, dz=0, dcore=0):
    moves = [
        ((x + dx) % 4 * 8 + (z + dz) % 4 * 2 + (core ^ dcore), x * 8 + z * 2 + core)
        for x in range(4)
        for z in range(4)
        for core in range(2)
    ]
    return lax.ppermute(value, "dev", moves)


def local(doc_states, context_embeds, w_qkv, w_out, ln_gain, queries, positive, lengths):
    docs, seq, hidden = doc_states.shape
    size = lax.axis_size("dev")
    me = lax.axis_index("dev")
    spot = jnp.stack([me >> 3, me & 1, (me >> 1) & 3])
    x = doc_states.reshape(docs * seq, hidden)
    arrays = (context_embeds, queries, w_qkv, w_out)
    got = fetch(build(give_kernel, 24, "give", spot, positive, *arrays), dcore=1)
    block = build(chip_kernel, 48, "chip", spot, positive, *arrays, got)
    four = jnp.stack([block] + [fetch(block, dx, dz) for dx, dz in SMALL[1:]])
    near = [four] + [fetch(four, dx, dz) for dx, dz in LARGE[1:]]
    far = [fetch(piece, dcore=1) for piece in near]
    embed, told = layer(lengths, spot, x, ln_gain, near + far, seq)
    embeds = spread_all(embed, "dev", size).reshape(size * docs, hidden)
    dgrad, qgrad, loss = contrast(spot, told, embeds, docs)
    return embed, dgrad, qgrad, loss.reshape(docs)


def solution(mesh):
    both = ("grp", "dev")
    return jax.shard_map(
        local,
        mesh=mesh,
        in_specs=(
            P(both, None, None),
            P(both, None),
            P("dev", None),
            P("dev", None),
            P(),
            P(both, None),
            P(both),
            P(both),
        ),
        out_specs=(P(both, None), P(both, None), P(both, None), P(both)),
        check_vma=False,
    )
```

```python
import functools

import jax
import jax.numpy as jnp
from jax import lax
from jax.experimental import pallas as pl
from jax.experimental.pallas import tpu as pltpu
from jax.sharding import PartitionSpec as P

HEAD = 64
PAIR = 128
SHARPNESS = 0.25
EPSILON = 1e-5
LOG2E = 1.4426950408889634
F32 = jnp.float32
BF16 = jnp.bfloat16
VMEM_LIMIT = 56 * 2**20
NT = (((1,), (1,)), ((), ()))


def halves(tile):
    low = lax.broadcasted_iota(jnp.int32, (1, PAIR), 1) < HEAD
    zero = jnp.zeros_like(tile)
    return jnp.where(low, tile, zero).astype(BF16), jnp.where(low, zero, tile).astype(BF16)


def ones_beside(rows):
    low = lax.broadcasted_iota(jnp.int32, (1, PAIR), 1) < HEAD
    first = lax.broadcasted_iota(jnp.int32, (2 * rows, 1), 0) < rows
    return jnp.where(jnp.logical_xor(first, low), 0.0, 1.0).astype(BF16)


HALF = 384
WEIGHTS = 3 * HALF
PROJECT = 4 * HALF
BLOCK = 5 * HALF
SMALL = ((0, 0), (2, 1), (0, 2), (2, 3))
LARGE = ((0, 0), (1, 0), (3, 0), (0, 1))


def half_block(half, context_ref, query_ref, wqkv_ref, wout_ref):
    hidden = query_ref.shape[1]
    first = half == 0
    parts = [wqkv_ref[:, b * hidden : (b + 1) * hidden].astype(F32) for b in range(3)] + [wout_ref[...].astype(F32)]
    parts.append(jnp.concatenate([context_ref[...].astype(F32), query_ref[...].astype(F32)], axis=0))
    parts = [jnp.where(first, p[:, :HALF], p[:, HALF:]) for p in parts]
    return jnp.concatenate(parts, axis=1)


def place_of_device():
    me = lax.axis_index("dev")
    return me >> 3, (me >> 1) & 3, me & 1


def give_kernel(context_ref, query_ref, wqkv_ref, wout_ref, o_ref):
    core = place_of_device()[2]
    o_ref[...] = half_block(1 - core, context_ref, query_ref, wqkv_ref, wout_ref).astype(BF16)


def chip_kernel(context_ref, query_ref, wqkv_ref, wout_ref, got_ref, o_ref):
    core = place_of_device()[2]
    own = half_block(core, context_ref, query_ref, wqkv_ref, wout_ref)
    got = got_ref[...].astype(F32)
    low = jnp.where(core == 0, own, got)
    high = jnp.where(core == 0, got, own)
    o_ref[:, :PROJECT] = jnp.concatenate([low[:, :PROJECT], high[:, :PROJECT]], axis=0).astype(BF16)
    rows = [low[:16, PROJECT:], high[:16, PROJECT:], low[16:, PROJECT:], high[16:, PROJECT:]]
    o_ref[:, PROJECT:] = jnp.concatenate(rows, axis=0).astype(BF16)


def build(kernel, rows, name, *arrays):
    vmem = pl.BlockSpec(memory_space=pltpu.VMEM)
    return pl.pallas_call(
        kernel,
        out_shape=jax.ShapeDtypeStruct((rows, BLOCK), BF16),
        in_specs=[vmem] * len(arrays),
        out_specs=vmem,
        name=name,
    )(*arrays)


def layer_kernel(rows, unroll, len_ref, positive_ref, x_ref, gain_ref, *refs):
    pieces, refs = refs[:8], refs[8:]
    o_ref, tell_ref, told_ref, w_s, wo_s, ctx_s, query_s, q_s, k_s, v_s, kc_s, vc_s, attn_s, sems = refs
    tokens, hidden = x_ref.shape
    docs = o_ref.shape[0]
    seq = tokens // docs
    pairs = hidden // PAIR
    per = HALF // PAIR
    nctx = ctx_s.shape[1] * ctx_s.shape[2]
    scale = LOG2E / HEAD**0.5
    x, z, core = place_of_device()
    weights, others, last = [], [], []
    for side in range(2):
        for p, (ax, az) in enumerate(LARGE):
            piece = pieces[side * 4 + p]
            n = side * 4 + p
            for k, (bx, bz) in enumerate(SMALL):
                chip = ((x + ax + bx) & 3) * 4 + ((z + az + bz) & 3)
                at = pl.multiple_of(chip * 48, 48)
                here = (core + side) & 1
                lanes = pl.ds(pl.multiple_of(here * HALF, HALF), HALF)
                weights.append(
                    pltpu.make_async_copy(
                        piece.at[k, :, pl.ds(0, WEIGHTS)], w_s.at[side, pl.ds(at, 48)], sems.at[0, n * 4 + k]
                    )
                )
                last.append(
                    pltpu.make_async_copy(
                        piece.at[k, :, pl.ds(WEIGHTS, HALF)], wo_s.at[pl.ds(at, 48), lanes], sems.at[1, n * 4 + k]
                    )
                )
                last.append(
                    pltpu.make_async_copy(
                        piece.at[k, pl.ds(32, 16), pl.ds(PROJECT, HALF)], query_s.at[side, chip], sems.at[2, n * 4 + k]
                    )
                )
            others.append(
                pltpu.make_async_copy(
                    piece.at[:, pl.ds(0, 32), pl.ds(PROJECT, HALF)], ctx_s.at[side, pl.ds(4 * p, 4)], sems.at[3, n]
                )
            )
    for copy in weights + others + last:
        copy.start()
    for copy in weights:
        copy.wait()

    def project(i, _):
        r = pl.ds(pl.multiple_of(i * rows, rows), rows)
        states = x_ref[r, :]
        for side in range(2):
            t = jnp.dot(states, w_s[side], preferred_element_type=F32)
            q_s[r, side * HALF : (side + 1) * HALF] = (t[:, :HALF] * scale).astype(BF16)
            for begin, out in ((HALF, k_s), (2 * HALF, v_s)):
                for j in range(per):
                    even, odd = halves(t[:, begin + j * PAIR : begin + (j + 1) * PAIR])
                    for e in range(rows // seq):
                        d = i * (rows // seq) + e
                        out[side * per + j, d, :seq] = even[e * seq : (e + 1) * seq]
                        out[side * per + j, d, seq:] = odd[e * seq : (e + 1) * seq]
        return 0

    lax.fori_loop(0, tokens // rows, project, 0)
    for copy in others:
        copy.wait()
    near = ctx_s[0].reshape(nctx, HALF)
    far = ctx_s[1].reshape(nctx, HALF)
    first = core == 0
    ctx = jnp.concatenate([jnp.where(first, near, far), jnp.where(first, far, near)], axis=1)
    for side in range(2):
        t = jnp.dot(ctx, w_s[side, :, HALF:], preferred_element_type=F32)
        for begin, out in ((0, kc_s), (HALF, vc_s)):
            for j in range(per):
                even, odd = halves(t[:, begin + j * PAIR : begin + (j + 1) * PAIR])
                out[side * per + j, :nctx] = even
                out[side * per + j, nctx:] = odd
    ones_ctx = ones_beside(nctx)
    ones_own = ones_beside(seq)
    slot = lax.broadcasted_iota(jnp.int32, (1, 2 * seq), 1)
    slot = jnp.where(slot < seq, slot, slot - seq)
    for j in range(pairs):

        def doc(d, _):
            r = pl.ds(pl.multiple_of(d * seq, seq), seq)
            q = q_s[r, j * PAIR : (j + 1) * PAIR]
            bias = jnp.where(slot < len_ref[d], 0.0, -jnp.inf).astype(F32)
            score_ctx = lax.dot_general(q, kc_s[j], NT, preferred_element_type=F32)
            score_own = lax.dot_general(q, k_s[j, d], NT, preferred_element_type=F32) + bias
            p_ctx, p_own = [], []
            for e in range(2):
                c = score_ctx[:, e * nctx : (e + 1) * nctx]
                o = score_own[:, e * seq : (e + 1) * seq]
                top = jnp.maximum(jnp.max(c, axis=1, keepdims=True), jnp.max(o, axis=1, keepdims=True))
                p_ctx.append(jnp.exp2(c - top).astype(BF16))
                p_own.append(jnp.exp2(o - top).astype(BF16))
            mixed = jnp.dot(
                jnp.concatenate(p_ctx, axis=1),
                jnp.concatenate([vc_s[j], ones_ctx], axis=1),
                preferred_element_type=F32,
            ) + jnp.dot(
                jnp.concatenate(p_own, axis=1),
                jnp.concatenate([v_s[j, d], ones_own], axis=1),
                preferred_element_type=F32,
            )
            here = pl.multiple_of(((core + j // per) & 1) * HALF + j % per * PAIR, PAIR)
            attn_s[r, pl.ds(here, PAIR)] = (mixed[:, :PAIR] / mixed[:, PAIR:]).astype(BF16)
            return 0

        lax.fori_loop(0, docs, doc, 0, unroll=unroll)
    for copy in last:
        copy.wait()
    position = lax.broadcasted_iota(jnp.int32, (seq, 1), 0)
    pooled = []
    for g in range(0, docs, 2):
        both = slice(g * seq, (g + 2) * seq)
        h_both = x_ref[both, :].astype(F32) + jnp.dot(attn_s[both, :], wo_s[...], preferred_element_type=F32)
        for d in (g, g + 1):
            h = h_both[(d - g) * seq : (d - g + 1) * seq]
            center = jnp.mean(h, axis=1, keepdims=True)
            off = h - center
            spread = jnp.mean(off * off, axis=1, keepdims=True)
            length = len_ref[d]
            weight = jnp.where(position < length, lax.rsqrt(spread + EPSILON), 0.0)
            pooled.append(jnp.sum(off * weight, axis=0, keepdims=True) / length.astype(F32))
    embed = jnp.concatenate(pooled, axis=0) * gain_ref[...]
    o_ref[...] = embed.astype(BF16)
    row = lax.broadcasted_iota(jnp.int32, (docs, 128), 0)
    beside = jnp.zeros((docs, 128), F32)
    for i in range(docs):
        beside = jnp.where(row == i, positive_ref[i].astype(F32), beside)
    tell = jnp.concatenate([embed, beside], axis=1).astype(BF16)
    for i in range(tell_ref.shape[0]):
        tell_ref[i] = tell
    count = told_ref.shape[0]
    near = query_s[0].reshape(count, HALF)
    far = query_s[1].reshape(count, HALF)
    told_ref[:, :HALF] = jnp.where(first, near, far)
    told_ref[:, HALF:] = jnp.where(first, far, near)


def layer(lengths, positive, x, gain, pieces, seq):
    tokens, hidden = x.shape
    docs = tokens // seq
    pairs = hidden // PAIR
    chips = 16
    nctx = chips * 32
    rows = 2 * seq
    vmem = pl.BlockSpec(memory_space=pltpu.VMEM)
    smem = pl.BlockSpec(memory_space=pltpu.SMEM)
    hbm = pl.BlockSpec(memory_space=pl.ANY)
    return pl.pallas_call(
        functools.partial(layer_kernel, rows, docs),
        out_shape=(
            jax.ShapeDtypeStruct((docs, hidden), BF16),
            jax.ShapeDtypeStruct((chips, docs, hidden + 128), BF16),
            jax.ShapeDtypeStruct((chips * 16, hidden), BF16),
        ),
        in_specs=[smem, smem, vmem, vmem] + [hbm] * 8,
        out_specs=(vmem, vmem, vmem),
        scratch_shapes=[
            pltpu.VMEM((2, hidden, WEIGHTS), BF16),
            pltpu.VMEM((hidden, hidden), BF16),
            pltpu.VMEM((2, chips, 32, HALF), BF16),
            pltpu.VMEM((2, chips, 16, HALF), BF16),
            pltpu.VMEM((tokens, hidden), BF16),
            pltpu.VMEM((pairs, docs, 2 * seq, PAIR), BF16),
            pltpu.VMEM((pairs, docs, 2 * seq, PAIR), BF16),
            pltpu.VMEM((pairs, 2 * nctx, PAIR), BF16),
            pltpu.VMEM((pairs, 2 * nctx, PAIR), BF16),
            pltpu.VMEM((tokens, hidden), BF16),
            pltpu.SemaphoreType.DMA((4, 32)),
        ],
        compiler_params=pltpu.CompilerParams(vmem_limit_bytes=VMEM_LIMIT),
        name="layer",
    )(lengths, positive, x, gain.reshape(1, hidden), *pieces)


def exact_dot(a, b):
    a1 = a.astype(BF16)
    rest = a - a1.astype(F32)
    a2 = rest.astype(BF16)
    a3 = (rest - a2.astype(F32)).astype(BF16)
    n = a.shape[0]
    out = jnp.dot(jnp.concatenate([a1, a2, a3], axis=0), b, preferred_element_type=F32)
    return out[:n] + out[n : 2 * n] + out[2 * n :]


def contrast_kernel(told_ref, near_ref, far_ref, dgrad_ref, qgrad_ref, loss_ref, coeff_s, rows_s, loss_s):
    docs, hidden = told_ref.shape
    chips, mine, _ = near_ref.shape
    divisor = 1.0 / (hidden**0.5 * SHARPNESS)
    x, z, core = place_of_device()
    near = near_ref[...].astype(F32)
    far = far_ref[...].astype(F32)
    low = jnp.where(core == 0, near, far)
    high = jnp.where(core == 0, far, near)
    table = jnp.concatenate([t[i] for i in range(chips) for t in (low, high)], axis=0)
    embed = table[:, :hidden].astype(BF16)
    beside = table[:, hidden:]
    positive = beside.T[:1]
    queries = told_ref[...]
    scores_t = lax.dot_general(embed, queries, NT, preferred_element_type=F32) * divisor
    top = jnp.max(scores_t, axis=0, keepdims=True)
    lse_t = top + jnp.log(jnp.sum(jnp.exp(scores_t - top), axis=0, keepdims=True))
    doc_id = lax.broadcasted_iota(jnp.int32, (docs, 1), 0).astype(F32)
    coeff_s[...] = jnp.exp(scores_t - lse_t) - jnp.where(doc_id == positive, 1.0, 0.0)
    chip = x * 4 + z
    own = pl.ds(pl.multiple_of((chip * 2 + core) * mine, mine), mine)
    dgrad_ref[...] = exact_dot(coeff_s[own, :], queries) * divisor
    both = told_ref[pl.ds(pl.multiple_of(chip * 16, 16), 16), :]
    scores = lax.dot_general(both, embed, NT, preferred_element_type=F32) * divisor
    rows_s[...] = scores
    loss_s[...] = beside
    scores = rows_s[pl.ds(pl.multiple_of(core * mine, mine), mine), :]
    own_positive = loss_s[own, :1]
    top = jnp.max(scores, axis=1, keepdims=True)
    lse = top + jnp.log(jnp.sum(jnp.exp(scores - top), axis=1, keepdims=True))
    is_positive = lax.broadcasted_iota(jnp.int32, (1, docs), 1).astype(F32) == own_positive
    loss = lse - jnp.sum(jnp.where(is_positive, scores, 0.0), axis=1, keepdims=True)
    coeff = jnp.exp(scores - lse) - jnp.where(is_positive, 1.0, 0.0)
    qgrad_ref[...] = exact_dot(coeff, embed) * divisor
    spot = lax.broadcasted_iota(jnp.int32, (mine, 128), 1)
    row = lax.broadcasted_iota(jnp.int32, (mine, 128), 0)
    loss_ref[...] = jnp.sum(jnp.where(spot == row, loss, 0.0), axis=0, keepdims=True)[:, :mine]


def contrast(told, near, far):
    docs, hidden = told.shape
    mine = near.shape[1]
    vmem = pl.BlockSpec(memory_space=pltpu.VMEM)
    return pl.pallas_call(
        contrast_kernel,
        out_shape=(
            jax.ShapeDtypeStruct((mine, hidden), F32),
            jax.ShapeDtypeStruct((mine, hidden), F32),
            jax.ShapeDtypeStruct((1, mine), F32),
        ),
        in_specs=[vmem, vmem, vmem],
        out_specs=(vmem, vmem, vmem),
        scratch_shapes=[
            pltpu.VMEM((docs, docs), F32),
            pltpu.VMEM((16, docs), F32),
            pltpu.VMEM((docs, 128), F32),
        ],
        compiler_params=pltpu.CompilerParams(vmem_limit_bytes=VMEM_LIMIT),
        name="contrast",
    )(told, near, far)


def fetch(value, dx=0, dz=0, dcore=0):
    moves = [
        ((x + dx) % 4 * 8 + (z + dz) % 4 * 2 + (core ^ dcore), x * 8 + z * 2 + core)
        for x in range(4)
        for z in range(4)
        for core in range(2)
    ]
    return lax.ppermute(value, "dev", moves)


def local(doc_states, context_embeds, w_qkv, w_out, ln_gain, queries, positive, lengths):
    docs, seq, hidden = doc_states.shape
    x = doc_states.reshape(docs * seq, hidden)
    arrays = (context_embeds, queries, w_qkv, w_out)
    got = fetch(build(give_kernel, 24, "give", *arrays), dcore=1)
    block = build(chip_kernel, 48, "chip", *arrays, got)
    four = jnp.stack([block] + [fetch(block, dx, dz) for dx, dz in SMALL[1:]])
    near = [four] + [fetch(four, dx, dz) for dx, dz in LARGE[1:]]
    far = [fetch(piece, dcore=1) for piece in near]
    embed, tell, told = layer(lengths, positive, x, ln_gain, near + far, seq)
    chips = [[chip * 2 + core for chip in range(16)] for core in range(2)]
    near = lax.all_to_all(tell, "dev", 0, 0, axis_index_groups=chips)
    far = fetch(near, dcore=1)
    dgrad, qgrad, loss = contrast(told, near, far)
    return embed, dgrad, qgrad, loss.reshape(docs)


def solution(mesh):
    both = ("grp", "dev")
    return jax.shard_map(
        local,
        mesh=mesh,
        in_specs=(
            P(both, None, None),
            P(both, None),
            P("dev", None),
            P("dev", None),
            P(),
            P(both, None),
            P(both),
            P(both),
        ),
        out_specs=(P(both, None), P(both, None), P(both, None), P(both)),
        check_vma=False,
    )
```

```python
import functools

import jax
import jax.numpy as jnp
from jax import lax
from jax.experimental import pallas as pl
from jax.experimental.pallas import tpu as pltpu
from jax.sharding import PartitionSpec as P

HEAD = 64
PAIR = 128
SHARPNESS = 0.25
EPSILON = 1e-5
LOG2E = 1.4426950408889634
F32 = jnp.float32
BF16 = jnp.bfloat16
NT = (((1,), (1,)), ((), ()))


def halves(tile):
    low = lax.broadcasted_iota(jnp.int32, (1, PAIR), 1) < HEAD
    zero = jnp.zeros_like(tile)
    return jnp.where(low, tile, zero).astype(BF16), jnp.where(low, zero, tile).astype(BF16)


def ones_beside(rows):
    low = lax.broadcasted_iota(jnp.int32, (1, PAIR), 1) < HEAD
    first = lax.broadcasted_iota(jnp.int32, (2 * rows, 1), 0) < rows
    return jnp.where(jnp.logical_xor(first, low), 0.0, 1.0).astype(BF16)


HALF = 384
WEIGHTS = 3 * HALF
PROJECT = 4 * HALF
BLOCK = 5 * HALF
SMALL = ((0, 0), (2, 1), (0, 2), (2, 3))
LARGE = ((0, 0), (1, 0), (3, 0), (0, 1))


def place_of_device():
    me = lax.axis_index("dev")
    return me >> 3, (me >> 1) & 3, me & 1


def cut_kernel(raw_ref, keep_ref, give_ref):
    first = place_of_device()[2] == 0
    for b in range(5):
        low = raw_ref[:, 2 * b * HALF : (2 * b + 1) * HALF].astype(F32)
        high = raw_ref[:, (2 * b + 1) * HALF : (2 * b + 2) * HALF].astype(F32)
        keep_ref[:, b * HALF : (b + 1) * HALF] = jnp.where(first, low, high).astype(BF16)
        give_ref[:, b * HALF : (b + 1) * HALF] = jnp.where(first, high, low).astype(BF16)


def cut(raw):
    vmem = pl.BlockSpec(memory_space=pltpu.VMEM)
    half = jax.ShapeDtypeStruct((raw.shape[0], BLOCK), BF16)
    return pl.pallas_call(
        cut_kernel,
        out_shape=(half, half),
        in_specs=[vmem],
        out_specs=(vmem, vmem),
        compiler_params=pltpu.CompilerParams(vmem_limit_bytes=4 * 2**20),
        name="cut",
    )(raw)


def chip_kernel(keep_ref, got_ref, o_ref):
    first = place_of_device()[2] == 0
    own = keep_ref[...].astype(F32)
    got = got_ref[...].astype(F32)
    low = jnp.where(first, own, got)
    high = jnp.where(first, got, own)
    o_ref[:, :PROJECT] = jnp.concatenate([low[:, :PROJECT], high[:, :PROJECT]], axis=0).astype(BF16)
    rows = [low[:16, PROJECT:], high[:16, PROJECT:], low[16:, PROJECT:], high[16:, PROJECT:]]
    o_ref[:, PROJECT:] = jnp.concatenate(rows, axis=0).astype(BF16)


def chip(keep, got):
    vmem = pl.BlockSpec(memory_space=pltpu.VMEM)
    return pl.pallas_call(
        chip_kernel,
        out_shape=jax.ShapeDtypeStruct((2 * keep.shape[0], BLOCK), BF16),
        in_specs=[vmem, vmem],
        out_specs=vmem,
        compiler_params=pltpu.CompilerParams(vmem_limit_bytes=4 * 2**20),
        name="chip",
    )(keep, got)


def layer_kernel(rows, unroll, len_ref, positive_ref, x_ref, gain_ref, *refs):
    pieces, refs = refs[:8], refs[8:]
    o_ref, tell_ref, told_ref, w_s, wo_s, ctx_s, query_s, told_s, q_s, k_s, v_s, kc_s, vc_s, attn_s, bias_s, sems = refs
    tokens, hidden = x_ref.shape
    docs = o_ref.shape[0]
    seq = tokens // docs
    pairs = hidden // PAIR
    per = HALF // PAIR
    nctx = ctx_s.shape[1] * ctx_s.shape[2]
    scale = LOG2E / HEAD**0.5
    x, z, core = place_of_device()
    weights, others, last, asked = ([], []), [], [], []
    for side in range(2):
        for p, (ax, az) in enumerate(LARGE):
            piece = pieces[side * 4 + p]
            n = side * 4 + p
            for k, (bx, bz) in enumerate(SMALL):
                chip = ((x + ax + bx) & 3) * 4 + ((z + az + bz) & 3)
                at = pl.multiple_of(chip * 48, 48)
                here = (core + side) & 1
                lanes = pl.ds(pl.multiple_of(here * HALF, HALF), HALF)
                weights[side].append(
                    pltpu.make_async_copy(
                        piece.at[k, :, pl.ds(0, WEIGHTS)], w_s.at[side, pl.ds(at, 48)], sems.at[0, n * 4 + k]
                    )
                )
                last.append(
                    pltpu.make_async_copy(
                        piece.at[k, :, pl.ds(WEIGHTS, HALF)], wo_s.at[pl.ds(at, 48), lanes], sems.at[1, n * 4 + k]
                    )
                )
                asked.append(
                    pltpu.make_async_copy(
                        piece.at[k, pl.ds(32, 16), pl.ds(PROJECT, HALF)], query_s.at[side, chip], sems.at[2, n * 4 + k]
                    )
                )
            others.append(
                pltpu.make_async_copy(
                    piece.at[:, pl.ds(0, 32), pl.ds(PROJECT, HALF)], ctx_s.at[side, pl.ds(4 * p, 4)], sems.at[3, n]
                )
            )
    for copy in weights[0] + others + weights[1] + asked:
        copy.start()

    def project(side, i, _):
        r = pl.ds(pl.multiple_of(i * rows, rows), rows)
        t = jnp.dot(x_ref[r, :], w_s[side], preferred_element_type=F32)
        q_s[r, side * HALF : (side + 1) * HALF] = (t[:, :HALF] * scale).astype(BF16)
        for begin, out in ((HALF, k_s), (2 * HALF, v_s)):
            for j in range(per):
                even, odd = halves(t[:, begin + j * PAIR : begin + (j + 1) * PAIR])
                for e in range(rows // seq):
                    d = i * (rows // seq) + e
                    out[side * per + j, d, :seq] = even[e * seq : (e + 1) * seq]
                    out[side * per + j, d, seq:] = odd[e * seq : (e + 1) * seq]
        return 0

    for side in range(2):
        for copy in weights[side]:
            copy.wait()
        lax.fori_loop(0, tokens // rows, functools.partial(project, side), 0)
    for copy in last:
        copy.start()
    for copy in others + asked:
        copy.wait()
    first = core == 0
    count = told_ref.shape[0]
    near = query_s[0].reshape(count, HALF)
    far = query_s[1].reshape(count, HALF)
    told_s[:, :HALF] = jnp.where(first, near, far)
    told_s[:, HALF:] = jnp.where(first, far, near)
    told_copy = pltpu.make_async_copy(told_s, told_ref, sems.at[3, 17])
    told_copy.start()
    near = ctx_s[0].reshape(nctx, HALF)
    far = ctx_s[1].reshape(nctx, HALF)
    ctx = jnp.concatenate([jnp.where(first, near, far), jnp.where(first, far, near)], axis=1)
    for side in range(2):
        t = jnp.dot(ctx, w_s[side, :, HALF:], preferred_element_type=F32)
        for begin, out in ((0, kc_s), (HALF, vc_s)):
            for j in range(per):
                even, odd = halves(t[:, begin + j * PAIR : begin + (j + 1) * PAIR])
                out[side * per + j, :nctx] = even
                out[side * per + j, nctx:] = odd
    ones_ctx = ones_beside(nctx)
    ones_own = ones_beside(seq)
    column = lax.broadcasted_iota(jnp.int32, (docs, docs), 0) == lax.broadcasted_iota(jnp.int32, (docs, docs), 1)

    def down(ref):
        return jnp.sum(jnp.where(column, ref[...].reshape(1, docs).astype(F32), 0.0), axis=1, keepdims=True)

    lengths = down(len_ref)
    slot = lax.broadcasted_iota(jnp.int32, (1, 2 * seq), 1)
    slot = jnp.where(slot < seq, slot, slot - seq).astype(F32)
    bias_s[...] = jnp.where(slot < lengths, 0.0, -jnp.inf)
    for j in range(pairs):

        def doc(d, _):
            r = pl.ds(pl.multiple_of(d * seq, seq), seq)
            q = q_s[r, j * PAIR : (j + 1) * PAIR]
            score_ctx = lax.dot_general(q, kc_s[j], NT, preferred_element_type=F32)
            score_own = lax.dot_general(q, k_s[j, d], NT, preferred_element_type=F32) + bias_s[pl.ds(d, 1), :]
            p_ctx, p_own = [], []
            for e in range(2):
                c = score_ctx[:, e * nctx : (e + 1) * nctx]
                o = score_own[:, e * seq : (e + 1) * seq]
                top = jnp.maximum(jnp.max(c, axis=1, keepdims=True), jnp.max(o, axis=1, keepdims=True))
                p_ctx.append(jnp.exp2(c - top).astype(BF16))
                p_own.append(jnp.exp2(o - top).astype(BF16))
            mixed = jnp.dot(
                jnp.concatenate(p_ctx, axis=1),
                jnp.concatenate([vc_s[j], ones_ctx], axis=1),
                preferred_element_type=F32,
            ) + jnp.dot(
                jnp.concatenate(p_own, axis=1),
                jnp.concatenate([v_s[j, d], ones_own], axis=1),
                preferred_element_type=F32,
            )
            here = pl.multiple_of(((core + j // per) & 1) * HALF + j % per * PAIR, PAIR)
            attn_s[r, pl.ds(here, PAIR)] = (mixed[:, :PAIR] / mixed[:, PAIR:]).astype(BF16)
            return 0

        lax.fori_loop(0, docs, doc, 0, unroll=unroll)
    for copy in last:
        copy.wait()
    position = lax.broadcasted_iota(jnp.int32, (seq, 1), 0).astype(F32)
    pooled = []
    for g in range(0, docs, 2):
        both = slice(g * seq, (g + 2) * seq)
        h_both = x_ref[both, :].astype(F32) + jnp.dot(attn_s[both, :], wo_s[...], preferred_element_type=F32)
        for d in (g, g + 1):
            h = h_both[(d - g) * seq : (d - g + 1) * seq]
            center = jnp.mean(h, axis=1, keepdims=True)
            off = h - center
            spread = jnp.mean(off * off, axis=1, keepdims=True)
            length = lengths[d : d + 1]
            weight = jnp.where(position < length, lax.rsqrt(spread + EPSILON), 0.0)
            pooled.append(jnp.sum(off * weight, axis=0, keepdims=True) / length)
    embed = jnp.concatenate(pooled, axis=0) * gain_ref[...].reshape(1, hidden)
    o_ref[...] = embed.astype(BF16)
    beside = jnp.broadcast_to(down(positive_ref), (docs, 128))
    tell = jnp.concatenate([embed, beside], axis=1).astype(BF16)
    for i in range(tell_ref.shape[0]):
        tell_ref[i] = tell
    told_copy.wait()


def layer(lengths, positive, x, gain, pieces, seq):
    tokens, hidden = x.shape
    docs = tokens // seq
    pairs = hidden // PAIR
    chips = 16
    nctx = chips * 32
    rows = 4 * seq
    vmem = pl.BlockSpec(memory_space=pltpu.VMEM)
    hbm = pl.BlockSpec(memory_space=pl.ANY)
    return pl.pallas_call(
        functools.partial(layer_kernel, rows, docs),
        out_shape=(
            jax.ShapeDtypeStruct((docs, hidden), BF16),
            jax.ShapeDtypeStruct((chips, docs, hidden + 128), BF16),
            jax.ShapeDtypeStruct((chips * 16, hidden), BF16),
        ),
        in_specs=[vmem, vmem, vmem, vmem] + [hbm] * 8,
        out_specs=(vmem, vmem, hbm),
        scratch_shapes=[
            pltpu.VMEM((2, hidden, WEIGHTS), BF16),
            pltpu.VMEM((hidden, hidden), BF16),
            pltpu.VMEM((2, chips, 32, HALF), BF16),
            pltpu.VMEM((2, chips, 16, HALF), BF16),
            pltpu.VMEM((chips * 16, hidden), BF16),
            pltpu.VMEM((tokens, hidden), BF16),
            pltpu.VMEM((pairs, docs, 2 * seq, PAIR), BF16),
            pltpu.VMEM((pairs, docs, 2 * seq, PAIR), BF16),
            pltpu.VMEM((pairs, 2 * nctx, PAIR), BF16),
            pltpu.VMEM((pairs, 2 * nctx, PAIR), BF16),
            pltpu.VMEM((tokens, hidden), BF16),
            pltpu.VMEM((docs, 2 * seq), F32),
            pltpu.SemaphoreType.DMA((4, 32)),
        ],
        compiler_params=pltpu.CompilerParams(vmem_limit_bytes=32 * 2**20),
        name="layer",
    )(lengths, positive, x, gain, *pieces)


def exact_dot(a, b):
    a1 = a.astype(BF16)
    rest = a - a1.astype(F32)
    a2 = rest.astype(BF16)
    a3 = (rest - a2.astype(F32)).astype(BF16)
    n = a.shape[0]
    out = jnp.dot(jnp.concatenate([a1, a2, a3], axis=0), b, preferred_element_type=F32)
    return out[:n] + out[n : 2 * n] + out[2 * n :]


def contrast_kernel(told_ref, near_ref, far_ref, dgrad_ref, qgrad_ref, loss_ref, coeff_s, rows_s, loss_s):
    docs, hidden = told_ref.shape
    chips, mine, _ = near_ref.shape
    divisor = 1.0 / (hidden**0.5 * SHARPNESS)
    x, z, core = place_of_device()
    near = near_ref[...].astype(F32)
    far = far_ref[...].astype(F32)
    low = jnp.where(core == 0, near, far)
    high = jnp.where(core == 0, far, near)
    table = jnp.concatenate([t[i] for i in range(chips) for t in (low, high)], axis=0)
    embed = table[:, :hidden].astype(BF16)
    beside = table[:, hidden:]
    positive = beside.T[:1]
    queries = told_ref[...]
    scores_t = lax.dot_general(embed, queries, NT, preferred_element_type=F32) * divisor
    top = jnp.max(scores_t, axis=0, keepdims=True)
    lse_t = top + jnp.log(jnp.sum(jnp.exp(scores_t - top), axis=0, keepdims=True))
    doc_id = lax.broadcasted_iota(jnp.int32, (docs, 1), 0).astype(F32)
    coeff_s[...] = jnp.exp(scores_t - lse_t) - jnp.where(doc_id == positive, 1.0, 0.0)
    chip = x * 4 + z
    own = pl.ds(pl.multiple_of((chip * 2 + core) * mine, mine), mine)
    dgrad_ref[...] = exact_dot(coeff_s[own, :], queries) * divisor
    both = told_ref[pl.ds(pl.multiple_of(chip * 16, 16), 16), :]
    scores = lax.dot_general(both, embed, NT, preferred_element_type=F32) * divisor
    rows_s[...] = scores
    loss_s[...] = beside
    scores = rows_s[pl.ds(pl.multiple_of(core * mine, mine), mine), :]
    own_positive = loss_s[own, :1]
    top = jnp.max(scores, axis=1, keepdims=True)
    lse = top + jnp.log(jnp.sum(jnp.exp(scores - top), axis=1, keepdims=True))
    is_positive = lax.broadcasted_iota(jnp.int32, (1, docs), 1).astype(F32) == own_positive
    loss = lse - jnp.sum(jnp.where(is_positive, scores, 0.0), axis=1, keepdims=True)
    coeff = jnp.exp(scores - lse) - jnp.where(is_positive, 1.0, 0.0)
    qgrad_ref[...] = exact_dot(coeff, embed) * divisor
    spot = lax.broadcasted_iota(jnp.int32, (mine, 128), 1)
    row = lax.broadcasted_iota(jnp.int32, (mine, 128), 0)
    loss_ref[...] = jnp.sum(jnp.where(spot == row, loss, 0.0), axis=0, keepdims=True)[:, :mine]


def contrast(told, near, far):
    docs, hidden = told.shape
    mine = near.shape[1]
    vmem = pl.BlockSpec(memory_space=pltpu.VMEM)
    return pl.pallas_call(
        contrast_kernel,
        out_shape=(
            jax.ShapeDtypeStruct((mine, hidden), F32),
            jax.ShapeDtypeStruct((mine, hidden), F32),
            jax.ShapeDtypeStruct((1, mine), F32),
        ),
        in_specs=[vmem, vmem, vmem],
        out_specs=(vmem, vmem, vmem),
        scratch_shapes=[
            pltpu.VMEM((docs, docs), F32),
            pltpu.VMEM((16, docs), F32),
            pltpu.VMEM((docs, 128), F32),
        ],
        compiler_params=pltpu.CompilerParams(vmem_limit_bytes=8 * 2**20),
        name="contrast",
    )(told, near, far)


def fetch(value, dx=0, dz=0, dcore=0):
    moves = [
        ((x + dx) % 4 * 8 + (z + dz) % 4 * 2 + (core ^ dcore), x * 8 + z * 2 + core)
        for x in range(4)
        for z in range(4)
        for core in range(2)
    ]
    return lax.ppermute(value, "dev", moves)


def local(doc_states, context_embeds, w_qkv, w_out, ln_gain, queries, positive, lengths):
    docs, seq, hidden = doc_states.shape
    x = doc_states.reshape(docs * seq, hidden)
    rows = jnp.concatenate([context_embeds, queries], axis=0)
    keep, give = cut(jnp.concatenate([w_qkv, w_out, rows], axis=1))
    block = chip(keep, fetch(give, dcore=1))
    four = jnp.stack([block] + [fetch(block, dx, dz) for dx, dz in SMALL[1:]])
    near = [four] + [fetch(four, dx, dz) for dx, dz in LARGE[1:]]
    far = [fetch(piece, dcore=1) for piece in near]
    embed, tell, told = layer(lengths, positive, x, ln_gain, near + far, seq)
    chips = [[chip * 2 + core for chip in range(16)] for core in range(2)]
    near = lax.all_to_all(tell, "dev", 0, 0, axis_index_groups=chips)
    far = fetch(near, dcore=1)
    dgrad, qgrad, loss = contrast(told, near, far)
    return embed, dgrad, qgrad, loss.reshape(docs)


def solution(mesh):
    both = ("grp", "dev")
    return jax.shard_map(
        local,
        mesh=mesh,
        in_specs=(
            P(both, None, None),
            P(both, None),
            P("dev", None),
            P("dev", None),
            P(),
            P(both, None),
            P(both),
            P(both),
        ),
        out_specs=(P(both, None), P(both, None), P(both, None), P(both)),
        check_vma=False,
    )
```

```python
import functools

import jax
import jax.numpy as jnp
from jax import lax
from jax.experimental import pallas as pl
from jax.experimental.pallas import tpu as pltpu
from jax.sharding import PartitionSpec as P

HEAD = 64
PAIR = 128
SHARPNESS = 0.25
EPSILON = 1e-5
LOG2E = 1.4426950408889634
F32 = jnp.float32
BF16 = jnp.bfloat16
NT = (((1,), (1,)), ((), ()))


def halves(tile):
    low = lax.broadcasted_iota(jnp.int32, (1, PAIR), 1) < HEAD
    zero = jnp.zeros_like(tile)
    return jnp.where(low, tile, zero).astype(BF16), jnp.where(low, zero, tile).astype(BF16)


def ones_beside(rows):
    low = lax.broadcasted_iota(jnp.int32, (1, PAIR), 1) < HEAD
    first = lax.broadcasted_iota(jnp.int32, (2 * rows, 1), 0) < rows
    return jnp.where(jnp.logical_xor(first, low), 0.0, 1.0).astype(BF16)


HALF = 384
WEIGHTS = 3 * HALF
PROJECT = 4 * HALF
BLOCK = 5 * HALF
SMALL = ((0, 0), (2, 1), (0, 2), (2, 3))
LARGE = ((0, 0), (1, 0), (3, 0), (0, 1))


def place_of_device():
    me = lax.axis_index("dev")
    return me >> 3, (me >> 1) & 3, me & 1


def cut_kernel(raw_ref, keep_ref, give_ref):
    first = place_of_device()[2] == 0
    for b in range(5):
        low = raw_ref[:, 2 * b * HALF : (2 * b + 1) * HALF].astype(F32)
        high = raw_ref[:, (2 * b + 1) * HALF : (2 * b + 2) * HALF].astype(F32)
        keep_ref[:, b * HALF : (b + 1) * HALF] = jnp.where(first, low, high).astype(BF16)
        give_ref[:, b * HALF : (b + 1) * HALF] = jnp.where(first, high, low).astype(BF16)


def cut(raw):
    vmem = pl.BlockSpec(memory_space=pltpu.VMEM)
    half = jax.ShapeDtypeStruct((raw.shape[0], BLOCK), BF16)
    return pl.pallas_call(
        cut_kernel,
        out_shape=(half, half),
        in_specs=[vmem],
        out_specs=(vmem, vmem),
        compiler_params=pltpu.CompilerParams(vmem_limit_bytes=4 * 2**20),
        name="cut",
    )(raw)


def chip_kernel(keep_ref, got_ref, o_ref):
    first = place_of_device()[2] == 0
    own = keep_ref[...].astype(F32)
    got = got_ref[...].astype(F32)
    low = jnp.where(first, own, got)
    high = jnp.where(first, got, own)
    o_ref[:, :PROJECT] = jnp.concatenate([low[:, :PROJECT], high[:, :PROJECT]], axis=0).astype(BF16)
    rows = [low[:16, PROJECT:], high[:16, PROJECT:], low[16:, PROJECT:], high[16:, PROJECT:]]
    o_ref[:, PROJECT:] = jnp.concatenate(rows, axis=0).astype(BF16)


def chip(keep, got):
    vmem = pl.BlockSpec(memory_space=pltpu.VMEM)
    return pl.pallas_call(
        chip_kernel,
        out_shape=jax.ShapeDtypeStruct((2 * keep.shape[0], BLOCK), BF16),
        in_specs=[vmem, vmem],
        out_specs=vmem,
        compiler_params=pltpu.CompilerParams(vmem_limit_bytes=4 * 2**20),
        name="chip",
    )(keep, got)


def layer_kernel(rows, unroll, len_ref, positive_ref, x_ref, gain_ref, *refs):
    pieces, refs = refs[:8], refs[8:]
    o_ref, tell_ref, told_ref, w_s, wo_s, ctx_s, query_s, told_s, q_s, k_s, v_s, kc_s, vc_s, attn_s, bias_s, sems = refs
    tokens, hidden = x_ref.shape
    docs = o_ref.shape[0]
    seq = tokens // docs
    pairs = hidden // PAIR
    per = HALF // PAIR
    nctx = ctx_s.shape[1] * ctx_s.shape[2]
    scale = LOG2E / HEAD**0.5
    x, z, core = place_of_device()
    weights, others, last, asked = ([], []), [], [], []
    for side in range(2):
        for p, (ax, az) in enumerate(LARGE):
            piece = pieces[side * 4 + p]
            n = side * 4 + p
            for k, (bx, bz) in enumerate(SMALL):
                chip = ((x + ax + bx) & 3) * 4 + (((z ^ az) + bz) & 3)
                at = pl.multiple_of(chip * 48, 48)
                here = (core + side) & 1
                lanes = pl.ds(pl.multiple_of(here * HALF, HALF), HALF)
                weights[side].append(
                    pltpu.make_async_copy(
                        piece.at[k, :, pl.ds(0, WEIGHTS)], w_s.at[side, pl.ds(at, 48)], sems.at[0, n * 4 + k]
                    )
                )
                last.append(
                    pltpu.make_async_copy(
                        piece.at[k, :, pl.ds(WEIGHTS, HALF)], wo_s.at[pl.ds(at, 48), lanes], sems.at[1, n * 4 + k]
                    )
                )
                asked.append(
                    pltpu.make_async_copy(
                        piece.at[k, pl.ds(32, 16), pl.ds(PROJECT, HALF)], query_s.at[side, chip], sems.at[2, n * 4 + k]
                    )
                )
            others.append(
                pltpu.make_async_copy(
                    piece.at[:, pl.ds(0, 32), pl.ds(PROJECT, HALF)], ctx_s.at[side, pl.ds(4 * p, 4)], sems.at[3, n]
                )
            )
    for copy in weights[0] + others + weights[1] + asked:
        copy.start()

    def project(side, i, _):
        r = pl.ds(pl.multiple_of(i * rows, rows), rows)
        t = jnp.dot(x_ref[r, :], w_s[side], preferred_element_type=F32)
        q_s[r, side * HALF : (side + 1) * HALF] = (t[:, :HALF] * scale).astype(BF16)
        for begin, out in ((HALF, k_s), (2 * HALF, v_s)):
            for j in range(per):
                even, odd = halves(t[:, begin + j * PAIR : begin + (j + 1) * PAIR])
                for e in range(rows // seq):
                    d = i * (rows // seq) + e
                    out[side * per + j, d, :seq] = even[e * seq : (e + 1) * seq]
                    out[side * per + j, d, seq:] = odd[e * seq : (e + 1) * seq]
        return 0

    for side in range(2):
        for copy in weights[side]:
            copy.wait()
        lax.fori_loop(0, tokens // rows, functools.partial(project, side), 0)
    for copy in last:
        copy.start()
    for copy in others + asked:
        copy.wait()
    first = core == 0
    count = told_ref.shape[0]
    near = query_s[0].reshape(count, HALF)
    far = query_s[1].reshape(count, HALF)
    told_s[:, :HALF] = jnp.where(first, near, far)
    told_s[:, HALF:] = jnp.where(first, far, near)
    told_copy = pltpu.make_async_copy(told_s, told_ref, sems.at[3, 17])
    told_copy.start()
    near = ctx_s[0].reshape(nctx, HALF)
    far = ctx_s[1].reshape(nctx, HALF)
    ctx = jnp.concatenate([jnp.where(first, near, far), jnp.where(first, far, near)], axis=1)
    for side in range(2):
        t = jnp.dot(ctx, w_s[side, :, HALF:], preferred_element_type=F32)
        for begin, out in ((0, kc_s), (HALF, vc_s)):
            for j in range(per):
                even, odd = halves(t[:, begin + j * PAIR : begin + (j + 1) * PAIR])
                out[side * per + j, :nctx] = even
                out[side * per + j, nctx:] = odd
    ones_ctx = ones_beside(nctx)
    ones_own = ones_beside(seq)
    column = lax.broadcasted_iota(jnp.int32, (docs, docs), 0) == lax.broadcasted_iota(jnp.int32, (docs, docs), 1)

    def down(ref):
        return jnp.sum(jnp.where(column, ref[...].reshape(1, docs).astype(F32), 0.0), axis=1, keepdims=True)

    lengths = down(len_ref)
    slot = lax.broadcasted_iota(jnp.int32, (1, 2 * seq), 1)
    slot = jnp.where(slot < seq, slot, slot - seq).astype(F32)
    bias_s[...] = jnp.where(slot < lengths, 0.0, -jnp.inf)
    for j in range(pairs):

        def doc(d, _):
            r = pl.ds(pl.multiple_of(d * seq, seq), seq)
            q = q_s[r, j * PAIR : (j + 1) * PAIR]
            score_ctx = lax.dot_general(q, kc_s[j], NT, preferred_element_type=F32)
            score_own = lax.dot_general(q, k_s[j, d], NT, preferred_element_type=F32) + bias_s[pl.ds(d, 1), :]
            p_ctx, p_own = [], []
            for e in range(2):
                c = score_ctx[:, e * nctx : (e + 1) * nctx]
                o = score_own[:, e * seq : (e + 1) * seq]
                top = jnp.maximum(jnp.max(c, axis=1, keepdims=True), jnp.max(o, axis=1, keepdims=True))
                p_ctx.append(jnp.exp2(c - top).astype(BF16))
                p_own.append(jnp.exp2(o - top).astype(BF16))
            mixed = jnp.dot(
                jnp.concatenate(p_ctx, axis=1),
                jnp.concatenate([vc_s[j], ones_ctx], axis=1),
                preferred_element_type=F32,
            ) + jnp.dot(
                jnp.concatenate(p_own, axis=1),
                jnp.concatenate([v_s[j, d], ones_own], axis=1),
                preferred_element_type=F32,
            )
            here = pl.multiple_of(((core + j // per) & 1) * HALF + j % per * PAIR, PAIR)
            attn_s[r, pl.ds(here, PAIR)] = (mixed[:, :PAIR] / mixed[:, PAIR:]).astype(BF16)
            return 0

        lax.fori_loop(0, docs, doc, 0, unroll=unroll)
    for copy in last:
        copy.wait()
    position = lax.broadcasted_iota(jnp.int32, (seq, 1), 0).astype(F32)
    pooled = []
    for g in range(0, docs, 2):
        both = slice(g * seq, (g + 2) * seq)
        h_both = x_ref[both, :].astype(F32) + jnp.dot(attn_s[both, :], wo_s[...], preferred_element_type=F32)
        for d in (g, g + 1):
            h = h_both[(d - g) * seq : (d - g + 1) * seq]
            center = jnp.mean(h, axis=1, keepdims=True)
            off = h - center
            spread = jnp.mean(off * off, axis=1, keepdims=True)
            length = lengths[d : d + 1]
            weight = jnp.where(position < length, lax.rsqrt(spread + EPSILON), 0.0)
            pooled.append(jnp.sum(off * weight, axis=0, keepdims=True) / length)
    embed = jnp.concatenate(pooled, axis=0) * gain_ref[...].reshape(1, hidden)
    o_ref[...] = embed.astype(BF16)
    beside = jnp.broadcast_to(down(positive_ref), (docs, 128))
    tell = jnp.concatenate([embed, beside], axis=1).astype(BF16)
    for i in range(tell_ref.shape[0]):
        tell_ref[i] = tell
    told_copy.wait()


def layer(lengths, positive, x, gain, pieces, seq):
    tokens, hidden = x.shape
    docs = tokens // seq
    pairs = hidden // PAIR
    chips = 16
    nctx = chips * 32
    rows = 4 * seq
    vmem = pl.BlockSpec(memory_space=pltpu.VMEM)
    hbm = pl.BlockSpec(memory_space=pl.ANY)
    return pl.pallas_call(
        functools.partial(layer_kernel, rows, docs),
        out_shape=(
            jax.ShapeDtypeStruct((docs, hidden), BF16),
            jax.ShapeDtypeStruct((chips, docs, hidden + 128), BF16),
            jax.ShapeDtypeStruct((chips * 16, hidden), BF16),
        ),
        in_specs=[vmem, vmem, vmem, vmem] + [hbm] * 8,
        out_specs=(vmem, vmem, hbm),
        scratch_shapes=[
            pltpu.VMEM((2, hidden, WEIGHTS), BF16),
            pltpu.VMEM((hidden, hidden), BF16),
            pltpu.VMEM((2, chips, 32, HALF), BF16),
            pltpu.VMEM((2, chips, 16, HALF), BF16),
            pltpu.VMEM((chips * 16, hidden), BF16),
            pltpu.VMEM((tokens, hidden), BF16),
            pltpu.VMEM((pairs, docs, 2 * seq, PAIR), BF16),
            pltpu.VMEM((pairs, docs, 2 * seq, PAIR), BF16),
            pltpu.VMEM((pairs, 2 * nctx, PAIR), BF16),
            pltpu.VMEM((pairs, 2 * nctx, PAIR), BF16),
            pltpu.VMEM((tokens, hidden), BF16),
            pltpu.VMEM((docs, 2 * seq), F32),
            pltpu.SemaphoreType.DMA((4, 32)),
        ],
        compiler_params=pltpu.CompilerParams(vmem_limit_bytes=32 * 2**20),
        name="layer",
    )(lengths, positive, x, gain, *pieces)


def exact_dot(a, b):
    a1 = a.astype(BF16)
    rest = a - a1.astype(F32)
    a2 = rest.astype(BF16)
    a3 = (rest - a2.astype(F32)).astype(BF16)
    n = a.shape[0]
    out = jnp.dot(jnp.concatenate([a1, a2, a3], axis=0), b, preferred_element_type=F32)
    return out[:n] + out[n : 2 * n] + out[2 * n :]


def contrast_kernel(told_ref, near_ref, far_ref, dgrad_ref, qgrad_ref, loss_ref, coeff_s, rows_s, loss_s):
    docs, hidden = told_ref.shape
    chips, mine, _ = near_ref.shape
    divisor = 1.0 / (hidden**0.5 * SHARPNESS)
    x, z, core = place_of_device()
    near = near_ref[...].astype(F32)
    far = far_ref[...].astype(F32)
    low = jnp.where(core == 0, near, far)
    high = jnp.where(core == 0, far, near)
    table = jnp.concatenate([t[i] for i in range(chips) for t in (low, high)], axis=0)
    embed = table[:, :hidden].astype(BF16)
    beside = table[:, hidden:]
    positive = beside.T[:1]
    queries = told_ref[...]
    scores_t = lax.dot_general(embed, queries, NT, preferred_element_type=F32) * divisor
    top = jnp.max(scores_t, axis=0, keepdims=True)
    lse_t = top + jnp.log(jnp.sum(jnp.exp(scores_t - top), axis=0, keepdims=True))
    doc_id = lax.broadcasted_iota(jnp.int32, (docs, 1), 0).astype(F32)
    coeff_s[...] = jnp.exp(scores_t - lse_t) - jnp.where(doc_id == positive, 1.0, 0.0)
    chip = x * 4 + z
    own = pl.ds(pl.multiple_of((chip * 2 + core) * mine, mine), mine)
    dgrad_ref[...] = exact_dot(coeff_s[own, :], queries) * divisor
    both = told_ref[pl.ds(pl.multiple_of(chip * 16, 16), 16), :]
    scores = lax.dot_general(both, embed, NT, preferred_element_type=F32) * divisor
    rows_s[...] = scores
    loss_s[...] = beside
    scores = rows_s[pl.ds(pl.multiple_of(core * mine, mine), mine), :]
    own_positive = loss_s[own, :1]
    top = jnp.max(scores, axis=1, keepdims=True)
    lse = top + jnp.log(jnp.sum(jnp.exp(scores - top), axis=1, keepdims=True))
    is_positive = lax.broadcasted_iota(jnp.int32, (1, docs), 1).astype(F32) == own_positive
    loss = lse - jnp.sum(jnp.where(is_positive, scores, 0.0), axis=1, keepdims=True)
    coeff = jnp.exp(scores - lse) - jnp.where(is_positive, 1.0, 0.0)
    qgrad_ref[...] = exact_dot(coeff, embed) * divisor
    spot = lax.broadcasted_iota(jnp.int32, (mine, 128), 1)
    row = lax.broadcasted_iota(jnp.int32, (mine, 128), 0)
    loss_ref[...] = jnp.sum(jnp.where(spot == row, loss, 0.0), axis=0, keepdims=True)[:, :mine]


def contrast(told, near, far):
    docs, hidden = told.shape
    mine = near.shape[1]
    vmem = pl.BlockSpec(memory_space=pltpu.VMEM)
    return pl.pallas_call(
        contrast_kernel,
        out_shape=(
            jax.ShapeDtypeStruct((mine, hidden), F32),
            jax.ShapeDtypeStruct((mine, hidden), F32),
            jax.ShapeDtypeStruct((1, mine), F32),
        ),
        in_specs=[vmem, vmem, vmem],
        out_specs=(vmem, vmem, vmem),
        scratch_shapes=[
            pltpu.VMEM((docs, docs), F32),
            pltpu.VMEM((16, docs), F32),
            pltpu.VMEM((docs, 128), F32),
        ],
        compiler_params=pltpu.CompilerParams(vmem_limit_bytes=8 * 2**20),
        name="contrast",
    )(told, near, far)


def fetch(value, dx=0, dz=0, pair=0, dcore=0):
    moves = [
        ((x + dx) % 4 * 8 + ((z ^ pair) + dz) % 4 * 2 + (core ^ dcore), x * 8 + z * 2 + core)
        for x in range(4)
        for z in range(4)
        for core in range(2)
    ]
    return lax.ppermute(value, "dev", moves)


def local(doc_states, context_embeds, w_qkv, w_out, ln_gain, queries, positive, lengths):
    docs, seq, hidden = doc_states.shape
    x = doc_states.reshape(docs * seq, hidden)
    rows = jnp.concatenate([context_embeds, queries], axis=0)
    keep, give = cut(jnp.concatenate([w_qkv, w_out, rows], axis=1))
    block = chip(keep, fetch(give, dcore=1))
    four = jnp.stack([block] + [fetch(block, dx, dz) for dx, dz in SMALL[1:]])
    near = [four] + [fetch(four, dx, pair=dz) for dx, dz in LARGE[1:]]
    far = [fetch(piece, dcore=1) for piece in near]
    embed, tell, told = layer(lengths, positive, x, ln_gain, near + far, seq)
    chips = [[chip * 2 + core for chip in range(16)] for core in range(2)]
    near = lax.all_to_all(tell, "dev", 0, 0, axis_index_groups=chips)
    far = fetch(near, dcore=1)
    dgrad, qgrad, loss = contrast(told, near, far)
    return embed, dgrad, qgrad, loss.reshape(docs)


def solution(mesh):
    both = ("grp", "dev")
    return jax.shard_map(
        local,
        mesh=mesh,
        in_specs=(
            P(both, None, None),
            P(both, None),
            P("dev", None),
            P("dev", None),
            P(),
            P(both, None),
            P(both),
            P(both),
        ),
        out_specs=(P(both, None), P(both, None), P(both, None), P(both)),
        check_vma=False,
    )
```

```python
import functools

import jax
import jax.numpy as jnp
from jax import lax
from jax.experimental import pallas as pl
from jax.experimental.pallas import tpu as pltpu
from jax.sharding import PartitionSpec as P

HEAD = 64
PAIR = 128
SHARPNESS = 0.25
EPSILON = 1e-5
LOG2E = 1.4426950408889634
F32 = jnp.float32
BF16 = jnp.bfloat16
NT = (((1,), (1,)), ((), ()))


def halves(tile):
    low = lax.broadcasted_iota(jnp.int32, (1, PAIR), 1) < HEAD
    zero = jnp.zeros_like(tile)
    return jnp.where(low, tile, zero).astype(BF16), jnp.where(low, zero, tile).astype(BF16)


def ones_beside(rows):
    low = lax.broadcasted_iota(jnp.int32, (1, PAIR), 1) < HEAD
    first = lax.broadcasted_iota(jnp.int32, (2 * rows, 1), 0) < rows
    return jnp.where(jnp.logical_xor(first, low), 0.0, 1.0).astype(BF16)


HALF = 384
WEIGHTS = 3 * HALF
PROJECT = 4 * HALF
BLOCK = 5 * HALF
SMALL = ((0, 0), (2, 1), (0, 2), (2, 3))
LARGE = ((0, 0), (1, 0), (3, 0), (0, 1))


def place_of_device():
    me = lax.axis_index("dev")
    return me >> 3, (me >> 1) & 3, me & 1


def cut_kernel(raw_ref, keep_ref, give_ref):
    first = place_of_device()[2] == 0
    for b in range(5):
        low = raw_ref[:, 2 * b * HALF : (2 * b + 1) * HALF].astype(F32)
        high = raw_ref[:, (2 * b + 1) * HALF : (2 * b + 2) * HALF].astype(F32)
        keep_ref[:, b * HALF : (b + 1) * HALF] = jnp.where(first, low, high).astype(BF16)
        give_ref[:, b * HALF : (b + 1) * HALF] = jnp.where(first, high, low).astype(BF16)


def cut(raw):
    vmem = pl.BlockSpec(memory_space=pltpu.VMEM)
    half = jax.ShapeDtypeStruct((raw.shape[0], BLOCK), BF16)
    return pl.pallas_call(
        cut_kernel,
        out_shape=(half, half),
        in_specs=[vmem],
        out_specs=(vmem, vmem),
        compiler_params=pltpu.CompilerParams(vmem_limit_bytes=4 * 2**20),
        name="cut",
    )(raw)


def chip_kernel(keep_ref, got_ref, o_ref):
    first = place_of_device()[2] == 0
    own = keep_ref[...].astype(F32)
    got = got_ref[...].astype(F32)
    low = jnp.where(first, own, got)
    high = jnp.where(first, got, own)
    o_ref[:, :PROJECT] = jnp.concatenate([low[:, :PROJECT], high[:, :PROJECT]], axis=0).astype(BF16)
    rows = [low[:16, PROJECT:], high[:16, PROJECT:], low[16:, PROJECT:], high[16:, PROJECT:]]
    o_ref[:, PROJECT:] = jnp.concatenate(rows, axis=0).astype(BF16)


def chip(keep, got):
    vmem = pl.BlockSpec(memory_space=pltpu.VMEM)
    return pl.pallas_call(
        chip_kernel,
        out_shape=jax.ShapeDtypeStruct((2 * keep.shape[0], BLOCK), BF16),
        in_specs=[vmem, vmem],
        out_specs=vmem,
        compiler_params=pltpu.CompilerParams(vmem_limit_bytes=4 * 2**20),
        name="chip",
    )(keep, got)


def layer_kernel(rows, unroll, len_ref, positive_ref, x_ref, gain_ref, *refs):
    pieces, rests, refs = refs[:8], refs[8:16], refs[16:]
    o_ref, tell_ref, told_ref, w_s, wo_s, ctx_s, query_s, told_s, q_s, k_s, v_s, kc_s, vc_s, attn_s, bias_s, sems = refs
    tokens, hidden = x_ref.shape
    docs = o_ref.shape[0]
    seq = tokens // docs
    pairs = hidden // PAIR
    per = HALF // PAIR
    nctx = ctx_s.shape[1] * ctx_s.shape[2]
    scale = LOG2E / HEAD**0.5
    x, z, core = place_of_device()
    weights, others, last, asked = ([], []), [], [], []
    for side in range(2):
        for p, (ax, az) in enumerate(LARGE):
            piece, rest = pieces[side * 4 + p], rests[side * 4 + p]
            n = side * 4 + p
            for k, (bx, bz) in enumerate(SMALL):
                chip = ((x + ax + bx) & 3) * 4 + (((z ^ az) + bz) & 3)
                at = pl.multiple_of(chip * 48, 48)
                here = (core + side) & 1
                lanes = pl.ds(pl.multiple_of(here * HALF, HALF), HALF)
                weights[side].append(
                    pltpu.make_async_copy(
                        piece.at[k, :, pl.ds(0, WEIGHTS)], w_s.at[side, pl.ds(at, 48)], sems.at[0, n * 4 + k]
                    )
                )
                last.append(
                    pltpu.make_async_copy(
                        rest.at[k, :, pl.ds(0, HALF)], wo_s.at[pl.ds(at, 48), lanes], sems.at[1, n * 4 + k]
                    )
                )
                asked.append(
                    pltpu.make_async_copy(
                        rest.at[k, pl.ds(32, 16), pl.ds(HALF, HALF)], query_s.at[side, chip], sems.at[2, n * 4 + k]
                    )
                )
            others.append(
                pltpu.make_async_copy(
                    rest.at[:, pl.ds(0, 32), pl.ds(HALF, HALF)], ctx_s.at[side, pl.ds(4 * p, 4)], sems.at[3, n]
                )
            )
    for copy in weights[0] + others + weights[1] + asked:
        copy.start()

    def project(side, i, _):
        r = pl.ds(pl.multiple_of(i * rows, rows), rows)
        t = jnp.dot(x_ref[r, :], w_s[side], preferred_element_type=F32)
        q_s[r, side * HALF : (side + 1) * HALF] = (t[:, :HALF] * scale).astype(BF16)
        for begin, out in ((HALF, k_s), (2 * HALF, v_s)):
            for j in range(per):
                even, odd = halves(t[:, begin + j * PAIR : begin + (j + 1) * PAIR])
                for e in range(rows // seq):
                    d = i * (rows // seq) + e
                    out[side * per + j, d, :seq] = even[e * seq : (e + 1) * seq]
                    out[side * per + j, d, seq:] = odd[e * seq : (e + 1) * seq]
        return 0

    for side in range(2):
        for copy in weights[side]:
            copy.wait()
        lax.fori_loop(0, tokens // rows, functools.partial(project, side), 0)
    for copy in last:
        copy.start()
    for copy in others + asked:
        copy.wait()
    first = core == 0
    count = told_ref.shape[0]
    near = query_s[0].reshape(count, HALF)
    far = query_s[1].reshape(count, HALF)
    told_s[:, :HALF] = jnp.where(first, near, far)
    told_s[:, HALF:] = jnp.where(first, far, near)
    told_copy = pltpu.make_async_copy(told_s, told_ref, sems.at[3, 17])
    told_copy.start()
    near = ctx_s[0].reshape(nctx, HALF)
    far = ctx_s[1].reshape(nctx, HALF)
    ctx = jnp.concatenate([jnp.where(first, near, far), jnp.where(first, far, near)], axis=1)
    for side in range(2):
        t = jnp.dot(ctx, w_s[side, :, HALF:], preferred_element_type=F32)
        for begin, out in ((0, kc_s), (HALF, vc_s)):
            for j in range(per):
                even, odd = halves(t[:, begin + j * PAIR : begin + (j + 1) * PAIR])
                out[side * per + j, :nctx] = even
                out[side * per + j, nctx:] = odd
    ones_ctx = ones_beside(nctx)
    ones_own = ones_beside(seq)
    column = lax.broadcasted_iota(jnp.int32, (docs, docs), 0) == lax.broadcasted_iota(jnp.int32, (docs, docs), 1)

    def down(ref):
        return jnp.sum(jnp.where(column, ref[...].reshape(1, docs).astype(F32), 0.0), axis=1, keepdims=True)

    lengths = down(len_ref)
    slot = lax.broadcasted_iota(jnp.int32, (1, 2 * seq), 1)
    slot = jnp.where(slot < seq, slot, slot - seq).astype(F32)
    bias_s[...] = jnp.where(slot < lengths, 0.0, -jnp.inf)
    for j in range(pairs):

        def doc(d, _):
            r = pl.ds(pl.multiple_of(d * seq, seq), seq)
            q = q_s[r, j * PAIR : (j + 1) * PAIR]
            score_ctx = lax.dot_general(q, kc_s[j], NT, preferred_element_type=F32)
            score_own = lax.dot_general(q, k_s[j, d], NT, preferred_element_type=F32) + bias_s[pl.ds(d, 1), :]
            p_ctx, p_own = [], []
            for e in range(2):
                c = score_ctx[:, e * nctx : (e + 1) * nctx]
                o = score_own[:, e * seq : (e + 1) * seq]
                top = jnp.maximum(jnp.max(c, axis=1, keepdims=True), jnp.max(o, axis=1, keepdims=True))
                p_ctx.append(jnp.exp2(c - top).astype(BF16))
                p_own.append(jnp.exp2(o - top).astype(BF16))
            mixed = jnp.dot(
                jnp.concatenate(p_ctx, axis=1),
                jnp.concatenate([vc_s[j], ones_ctx], axis=1),
                preferred_element_type=F32,
            ) + jnp.dot(
                jnp.concatenate(p_own, axis=1),
                jnp.concatenate([v_s[j, d], ones_own], axis=1),
                preferred_element_type=F32,
            )
            here = pl.multiple_of(((core + j // per) & 1) * HALF + j % per * PAIR, PAIR)
            attn_s[r, pl.ds(here, PAIR)] = (mixed[:, :PAIR] / mixed[:, PAIR:]).astype(BF16)
            return 0

        lax.fori_loop(0, docs, doc, 0, unroll=unroll)
    for copy in last:
        copy.wait()
    position = lax.broadcasted_iota(jnp.int32, (seq, 1), 0).astype(F32)
    pooled = []
    for g in range(0, docs, 2):
        both = slice(g * seq, (g + 2) * seq)
        h_both = x_ref[both, :].astype(F32) + jnp.dot(attn_s[both, :], wo_s[...], preferred_element_type=F32)
        for d in (g, g + 1):
            h = h_both[(d - g) * seq : (d - g + 1) * seq]
            center = jnp.mean(h, axis=1, keepdims=True)
            off = h - center
            spread = jnp.mean(off * off, axis=1, keepdims=True)
            length = lengths[d : d + 1]
            weight = jnp.where(position < length, lax.rsqrt(spread + EPSILON), 0.0)
            pooled.append(jnp.sum(off * weight, axis=0, keepdims=True) / length)
    embed = jnp.concatenate(pooled, axis=0) * gain_ref[...].reshape(1, hidden)
    o_ref[...] = embed.astype(BF16)
    beside = jnp.broadcast_to(down(positive_ref), (docs, 128))
    tell = jnp.concatenate([embed, beside], axis=1).astype(BF16)
    for i in range(tell_ref.shape[0]):
        tell_ref[i] = tell
    told_copy.wait()


def layer(lengths, positive, x, gain, pieces, seq):
    tokens, hidden = x.shape
    docs = tokens // seq
    pairs = hidden // PAIR
    chips = 16
    nctx = chips * 32
    rows = 4 * seq
    vmem = pl.BlockSpec(memory_space=pltpu.VMEM)
    hbm = pl.BlockSpec(memory_space=pl.ANY)
    return pl.pallas_call(
        functools.partial(layer_kernel, rows, docs),
        out_shape=(
            jax.ShapeDtypeStruct((docs, hidden), BF16),
            jax.ShapeDtypeStruct((chips, docs, hidden + 128), BF16),
            jax.ShapeDtypeStruct((chips * 16, hidden), BF16),
        ),
        in_specs=[vmem, vmem, vmem, vmem] + [hbm] * 16,
        out_specs=(vmem, vmem, hbm),
        scratch_shapes=[
            pltpu.VMEM((2, hidden, WEIGHTS), BF16),
            pltpu.VMEM((hidden, hidden), BF16),
            pltpu.VMEM((2, chips, 32, HALF), BF16),
            pltpu.VMEM((2, chips, 16, HALF), BF16),
            pltpu.VMEM((chips * 16, hidden), BF16),
            pltpu.VMEM((tokens, hidden), BF16),
            pltpu.VMEM((pairs, docs, 2 * seq, PAIR), BF16),
            pltpu.VMEM((pairs, docs, 2 * seq, PAIR), BF16),
            pltpu.VMEM((pairs, 2 * nctx, PAIR), BF16),
            pltpu.VMEM((pairs, 2 * nctx, PAIR), BF16),
            pltpu.VMEM((tokens, hidden), BF16),
            pltpu.VMEM((docs, 2 * seq), F32),
            pltpu.SemaphoreType.DMA((4, 32)),
        ],
        compiler_params=pltpu.CompilerParams(vmem_limit_bytes=32 * 2**20),
        name="layer",
    )(lengths, positive, x, gain, *pieces)


def exact_dot(a, b):
    a1 = a.astype(BF16)
    rest = a - a1.astype(F32)
    a2 = rest.astype(BF16)
    a3 = (rest - a2.astype(F32)).astype(BF16)
    n = a.shape[0]
    out = jnp.dot(jnp.concatenate([a1, a2, a3], axis=0), b, preferred_element_type=F32)
    return out[:n] + out[n : 2 * n] + out[2 * n :]


def contrast_kernel(told_ref, near_ref, far_ref, dgrad_ref, qgrad_ref, loss_ref, coeff_s, rows_s, loss_s):
    docs, hidden = told_ref.shape
    chips, mine, _ = near_ref.shape
    divisor = 1.0 / (hidden**0.5 * SHARPNESS)
    x, z, core = place_of_device()
    near = near_ref[...].astype(F32)
    far = far_ref[...].astype(F32)
    low = jnp.where(core == 0, near, far)
    high = jnp.where(core == 0, far, near)
    table = jnp.concatenate([t[i] for i in range(chips) for t in (low, high)], axis=0)
    embed = table[:, :hidden].astype(BF16)
    beside = table[:, hidden:]
    positive = beside.T[:1]
    queries = told_ref[...]
    scores_t = lax.dot_general(embed, queries, NT, preferred_element_type=F32) * divisor
    top = jnp.max(scores_t, axis=0, keepdims=True)
    lse_t = top + jnp.log(jnp.sum(jnp.exp(scores_t - top), axis=0, keepdims=True))
    doc_id = lax.broadcasted_iota(jnp.int32, (docs, 1), 0).astype(F32)
    coeff_s[...] = jnp.exp(scores_t - lse_t) - jnp.where(doc_id == positive, 1.0, 0.0)
    chip = x * 4 + z
    own = pl.ds(pl.multiple_of((chip * 2 + core) * mine, mine), mine)
    dgrad_ref[...] = exact_dot(coeff_s[own, :], queries) * divisor
    both = told_ref[pl.ds(pl.multiple_of(chip * 16, 16), 16), :]
    scores = lax.dot_general(both, embed, NT, preferred_element_type=F32) * divisor
    rows_s[...] = scores
    loss_s[...] = beside
    scores = rows_s[pl.ds(pl.multiple_of(core * mine, mine), mine), :]
    own_positive = loss_s[own, :1]
    top = jnp.max(scores, axis=1, keepdims=True)
    lse = top + jnp.log(jnp.sum(jnp.exp(scores - top), axis=1, keepdims=True))
    is_positive = lax.broadcasted_iota(jnp.int32, (1, docs), 1).astype(F32) == own_positive
    loss = lse - jnp.sum(jnp.where(is_positive, scores, 0.0), axis=1, keepdims=True)
    coeff = jnp.exp(scores - lse) - jnp.where(is_positive, 1.0, 0.0)
    qgrad_ref[...] = exact_dot(coeff, embed) * divisor
    spot = lax.broadcasted_iota(jnp.int32, (mine, 128), 1)
    row = lax.broadcasted_iota(jnp.int32, (mine, 128), 0)
    loss_ref[...] = jnp.sum(jnp.where(spot == row, loss, 0.0), axis=0, keepdims=True)[:, :mine]


def contrast(told, near, far):
    docs, hidden = told.shape
    mine = near.shape[1]
    vmem = pl.BlockSpec(memory_space=pltpu.VMEM)
    return pl.pallas_call(
        contrast_kernel,
        out_shape=(
            jax.ShapeDtypeStruct((mine, hidden), F32),
            jax.ShapeDtypeStruct((mine, hidden), F32),
            jax.ShapeDtypeStruct((1, mine), F32),
        ),
        in_specs=[vmem, vmem, vmem],
        out_specs=(vmem, vmem, vmem),
        scratch_shapes=[
            pltpu.VMEM((docs, docs), F32),
            pltpu.VMEM((16, docs), F32),
            pltpu.VMEM((docs, 128), F32),
        ],
        compiler_params=pltpu.CompilerParams(vmem_limit_bytes=8 * 2**20),
        name="contrast",
    )(told, near, far)


def fetch(value, dx=0, dz=0, pair=0, dcore=0):
    moves = [
        ((x + dx) % 4 * 8 + ((z ^ pair) + dz) % 4 * 2 + (core ^ dcore), x * 8 + z * 2 + core)
        for x in range(4)
        for z in range(4)
        for core in range(2)
    ]
    return lax.ppermute(value, "dev", moves)


def local(doc_states, context_embeds, w_qkv, w_out, ln_gain, queries, positive, lengths):
    docs, seq, hidden = doc_states.shape
    x = doc_states.reshape(docs * seq, hidden)
    rows = jnp.concatenate([context_embeds, queries], axis=0)
    keep, give = cut(jnp.concatenate([w_qkv, w_out, rows], axis=1))
    block = chip(keep, fetch(give, dcore=1))
    four = jnp.stack([block] + [fetch(block, dx, dz) for dx, dz in SMALL[1:]])
    gathered = []
    for part in (four[:, :, :WEIGHTS], four[:, :, WEIGHTS:]):
        near = [part] + [fetch(part, dx, pair=dz) for dx, dz in LARGE[1:]]
        gathered += near + [fetch(piece, dcore=1) for piece in near]
    embed, tell, told = layer(lengths, positive, x, ln_gain, gathered, seq)
    chips = [[chip * 2 + core for chip in range(16)] for core in range(2)]
    near = lax.all_to_all(tell, "dev", 0, 0, axis_index_groups=chips)
    far = fetch(near, dcore=1)
    dgrad, qgrad, loss = contrast(told, near, far)
    return embed, dgrad, qgrad, loss.reshape(docs)


def solution(mesh):
    both = ("grp", "dev")
    return jax.shard_map(
        local,
        mesh=mesh,
        in_specs=(
            P(both, None, None),
            P(both, None),
            P("dev", None),
            P("dev", None),
            P(),
            P(both, None),
            P(both),
            P(both),
        ),
        out_specs=(P(both, None), P(both, None), P(both, None), P(both)),
        check_vma=False,
    )
```
